32 devices in a mesh: group: 4 (over y, x), tp: 8 (over z, core).
Axes of the slice: x: 2, y: 2, z: 4, core: 2. Of those that a mesh axis runs over, the one named last changes fastest.
Arguments:
- decoding_input: bfloat16 [8, 8, 5120], P('group'), may hold values from -6 to 6
- query_weight: bfloat16 [5120, 1024], P(None, 'tp'), may hold values from -0.078125 to 0.078125
- output_weight: bfloat16 [1024, 5120], P('tp'), may hold values from -0.25 to 0.25
- query_down_factor: bfloat16 [5120, 64], P('tp', 'group'), may hold values from -0.078125 to 0.078125
- query_up_factor: bfloat16 [64, 1024], P('group', 'tp'), may hold values from -0.75 to 0.75
- output_down_factor: bfloat16 [1024, 64], P('tp', 'group'), may hold values from -0.1875 to 0.1875
- output_up_factor: bfloat16 [64, 5120], P('group', 'tp'), may hold values from -0.75 to 0.75
- stored_keys: bfloat16 [8, 1, 2048, 128], P('group', None, 'tp')
- stored_values: bfloat16 [8, 1, 2048, 128], P('group', None, 'tp'), may hold values from -96 to 96
- current_keys: bfloat16 [8, 8, 1, 128], P('group'), may hold values from -6 to 6
- current_values: bfloat16 [8, 8, 1, 128], P('group'), may hold values from -96 to 96
- lengths: int32 [8], P('group'), may hold values from 1 to 2048, 8192 in all
Outputs:
- attended: bfloat16 [8, 8, 5120], P('group', None, 'tp')
The draws below stay inside these ranges and needn't reach their ends.
All inputs are finite; a program needn't handle non-finite values. No bound on the sum of `lengths` on one device may be relied on, other than what follows from the above.
Results may differ from the reference program's by a relative error of at most 0.0085.
The reference program's roundings to bfloat16 on the way count: a program that leaves them out, or rounds other values in their place, can miss the bound.
Values may be sent and summed in bfloat16 or wider, within the bound.
A program may use at most 64 MiB of HBM per device.

```python
import math
import jax
import jax.numpy as jnp
import numpy as np
from jax import lax

MODEL_DIM = 5120
HEAD_DIM = 128
ADAPTER_RANK = 64
STEPS = 8
CACHE = 2048
QUERY_HEADS = 8
KVH = 1
ROWS = 8
N_TP = 8


def draw_stored_keys(key, part):
    key = jax.random.fold_in(key, 11)
    normals = jnp.clip(jax.random.normal(key, (ROWS, KVH, CACHE, HEAD_DIM), jnp.float32), -6.0, 6.0)
    return normals.astype(jnp.bfloat16)


def raised(values, rng, source, target, shards_of, factor):
    owner, partner = [(jnp.arange(values.shape[axis_at]) // (values.shape[axis_at] // shards_of)).reshape([-1 if axis == axis_at else 1 for axis in range(values.ndim)]) for axis_at in (source, target)]
    chosen = jax.random.permutation(rng, shards_of)[partner]
    strong = (owner == chosen) | (owner == (partner + shards_of // 2) % shards_of)
    return jnp.where(strong, factor * values, values)


def levels(rng, extent, cuts, smallest, top_value):
    level, own = 1.0, jax.random.fold_in(rng, 6)
    for axis_at, shards_of in cuts:
        steps = jnp.exp(jax.random.uniform(jax.random.fold_in(own, axis_at), (shards_of,), jnp.float32, smallest / len(cuts), top_value / len(cuts)))
        level = level * jnp.repeat(steps, extent[axis_at] // shards_of).reshape([-1 if axis == axis_at else 1 for axis in range(len(extent))])
    return level


def length_profile(count, total, bound, lean):
    loads = [(1 << 20) // math.isqrt(grade ** lean) + 1 for grade in range(2, count + 1)]
    spare, holding = total - bound - (count - 1), [1] * (count - 1)
    while spare > 0:
        candidates = [i for i in range(count - 1) if holding[i] < bound]
        whole, left = sum([loads[i] for i in candidates]), spare
        for i in candidates:
            addition = min(bound - holding[i], max(1, left * loads[i] // whole), spare)
            holding[i] = holding[i] + addition
            spare = spare - addition
    return np.array([bound] + holding)


def uneven(rng, count, total, reach, slope):
    if count == 2:
        one = jax.random.randint(rng, (), max(1, total - reach), min(reach, total - 1) + 1)
        return jnp.stack([one, total - one])
    sizes = jnp.asarray(length_profile(count, total, reach, slope), jnp.int32)
    couples = (count - 1) // 2
    donor, taker = sizes[1:1 + 2 * couples:2], sizes[2:2 + 2 * couples:2]
    room = jnp.minimum(donor - 1, reach - taker)
    shifted = jax.random.randint(jax.random.fold_in(rng, 1), (couples,), 0, 1 << 20) % (room + 1)
    sizes = sizes.at[1:1 + 2 * couples:2].set(donor - shifted).at[2:2 + 2 * couples:2].set(taker + shifted)
    return sizes[jax.random.permutation(jax.random.fold_in(rng, 2), count)]


def noise(own_key, extent, spread, most, cuts=(), held_as=jnp.bfloat16):
    drawn = spread * jax.random.normal(own_key, extent, jnp.float32)
    if cuts:
        drawn = drawn * levels(own_key, extent, cuts, -0.22, 0.18)
    return jnp.clip(drawn, -most, most).astype(held_as)


def bell_draw_with(key, extent, deviation, reach, split, heavy, dtype=jnp.bfloat16):
    values = deviation * jax.random.normal(key, extent, jnp.float32)
    if split:
        values = values * levels(key, extent, split, -0.22, 0.18)
    return jnp.clip(raised(values, jax.random.fold_in(key, 3), *heavy), -reach, reach).astype(dtype)


def setup_inputs(seed: int = 0) -> dict:
    seeds = jax.random.split(jax.random.key(seed), 13)
    decoding_input = noise(seeds[0], (ROWS, STEPS, MODEL_DIM), 1.0, 6.0, ((0, 4),))
    query_weight = noise(seeds[1], (MODEL_DIM, QUERY_HEADS * HEAD_DIM), MODEL_DIM ** -0.5, 0.078125, ((1, 8),))
    output_weight = bell_draw_with(seeds[2], (QUERY_HEADS * HEAD_DIM, MODEL_DIM), (QUERY_HEADS * HEAD_DIM) ** -0.5, 0.25, ((0, 8),), (0, 1, 8, 2.0))
    query_down_factor = noise(seeds[3], (MODEL_DIM, ADAPTER_RANK), MODEL_DIM ** -0.5, 0.078125, ((0, 8), (1, 4)))
    query_up_factor = noise(seeds[4], (ADAPTER_RANK, QUERY_HEADS * HEAD_DIM), ADAPTER_RANK ** -0.5, 0.75, ((0, 4), (1, 8)))
    output_down_factor = noise(seeds[5], (QUERY_HEADS * HEAD_DIM, ADAPTER_RANK), (QUERY_HEADS * HEAD_DIM) ** -0.5, 0.1875, ((0, 8), (1, 4)))
    output_up_factor = noise(seeds[6], (ADAPTER_RANK, MODEL_DIM), ADAPTER_RANK ** -0.5, 0.75, ((0, 4), (1, 8)))
    stored_keys = draw_stored_keys(jax.random.fold_in(seeds[12], 71), 0)
    stored_values = noise(seeds[8], (ROWS, KVH, CACHE, HEAD_DIM), 16.0, 96.0, ((0, 4), (2, 8)))
    current_keys = noise(seeds[9], (ROWS, STEPS, KVH, HEAD_DIM), 1.0, 6.0, ((0, 4),))
    current_values = noise(seeds[10], (ROWS, STEPS, KVH, HEAD_DIM), 16.0, 96.0, ((0, 4),))
    lengths = uneven(seeds[11], ROWS, ROWS * CACHE // 2, CACHE, 0).astype(jnp.int32)
    return dict(decoding_input=decoding_input, query_weight=query_weight, output_weight=output_weight, query_down_factor=query_down_factor, query_up_factor=query_up_factor, output_down_factor=output_down_factor, output_up_factor=output_up_factor, stored_keys=stored_keys, stored_values=stored_values, current_keys=current_keys, current_values=current_values, lengths=lengths)


masked_score = -1e30


def reference(decoding_input, query_weight, output_weight, query_down_factor, query_up_factor, output_down_factor, output_up_factor, stored_keys, stored_values, current_keys, current_values, lengths):
    highest_precision = lax.Precision.HIGHEST
    flattened_input = decoding_input.reshape(ROWS * STEPS, MODEL_DIM)
    adapter_rank_input = jnp.dot(flattened_input, query_down_factor, preferred_element_type=jnp.float32)
    query_rows = jnp.dot(flattened_input, query_weight, preferred_element_type=jnp.float32) + 2.0 * jnp.dot(adapter_rank_input, query_up_factor.astype(jnp.float32), precision=highest_precision)
    query_rows = query_rows.astype(jnp.bfloat16).reshape(ROWS, STEPS, QUERY_HEADS, HEAD_DIM)
    group_heads = QUERY_HEADS // KVH
    block_size = CACHE // N_TP
    score_scale = HEAD_DIM ** -0.5

    def one_row(items):
        row_queries, row_keys, row_values, fresh_keys, fresh_values, row_length = items
        grouped = row_queries.astype(jnp.float32).reshape(STEPS, KVH, group_heads, HEAD_DIM)
        scores = jnp.einsum("skgd,kcd->skgc", grouped, row_keys.astype(jnp.float32), precision=highest_precision) * score_scale
        scores = scores.reshape(STEPS, QUERY_HEADS, N_TP, block_size)
        visible = (lax.iota(jnp.int32, CACHE) < row_length).reshape(N_TP, block_size)
        peaks = jnp.max(jnp.where(visible, scores, masked_score), axis=-1)
        weights = jnp.where(visible, jnp.exp(scores - peaks[..., None]), 0.0)
        weight_sums = jnp.sum(weights, axis=-1)
        rounded = lax.optimization_barrier(weights.astype(jnp.bfloat16)).astype(jnp.float32)
        blocked_values = row_values.astype(jnp.float32).reshape(KVH, N_TP, block_size, HEAD_DIM)
        outputs = jnp.einsum("skgbc,kbcd->skgbd", rounded.reshape(STEPS, KVH, group_heads, N_TP, block_size), blocked_values, precision=highest_precision)
        outputs = outputs.reshape(STEPS, QUERY_HEADS, N_TP, HEAD_DIM)
        cache_peak = jnp.max(peaks, axis=-1)
        factor = jnp.exp(peaks - cache_peak[..., None])
        cache_sum = jnp.sum(weight_sums * factor, axis=-1)
        cache_out = jnp.sum(outputs * factor[..., None], axis=2)
        fresh_scores = jnp.einsum("skgd,tkd->skgt", grouped, fresh_keys.astype(jnp.float32), precision=highest_precision).reshape(STEPS, QUERY_HEADS, STEPS) * score_scale
        order = lax.iota(jnp.int32, STEPS)
        causal = (order[:, None] >= order[None, :])[:, None, :]
        fresh_peak = jnp.max(jnp.where(causal, fresh_scores, masked_score), axis=-1)
        fresh_weights = jnp.where(causal, jnp.exp(fresh_scores - fresh_peak[..., None]), 0.0)
        fresh_sum = jnp.sum(fresh_weights, axis=-1)
        fresh_rounded = lax.optimization_barrier(fresh_weights.astype(jnp.bfloat16)).astype(jnp.float32)
        fresh_out = jnp.einsum("skgt,tkd->skgd", fresh_rounded.reshape(STEPS, KVH, group_heads, STEPS), fresh_values.astype(jnp.float32), precision=highest_precision).reshape(STEPS, QUERY_HEADS, HEAD_DIM)
        joint_peak = jnp.maximum(cache_peak, fresh_peak)
        left = jnp.exp(cache_peak - joint_peak)
        right = jnp.exp(fresh_peak - joint_peak)
        numer = cache_out * left[..., None] + fresh_out * right[..., None]
        denom = cache_sum * left + fresh_sum * right
        return (numer / denom[..., None]).astype(jnp.bfloat16)

    context_rows = lax.map(one_row, (query_rows, stored_keys, stored_values, current_keys, current_values, lengths))
    context_rows = context_rows.reshape(ROWS * STEPS, QUERY_HEADS * HEAD_DIM)
    base_output = jnp.dot(context_rows, output_weight, preferred_element_type=jnp.float32)
    adapter_rank_output = jnp.dot(context_rows, output_down_factor, preferred_element_type=jnp.float32)
    attended = base_output + 2.0 * jnp.dot(adapter_rank_output, output_up_factor.astype(jnp.float32), precision=highest_precision)
    return attended.astype(jnp.bfloat16).reshape(ROWS, STEPS, MODEL_DIM)
```

```python
import functools

import jax
import jax.numpy as jnp
from jax import lax
from jax.experimental import pallas as pl
from jax.experimental.pallas import tpu as pltpu
from jax.sharding import PartitionSpec as P

adapter_scale = 2.0
masked_score = -1e30
f32 = jnp.float32
bf16 = jnp.bfloat16
MESH = pl.DeviceIdType.MESH
RANK_TILE = 16
LANES = 128


def rounded_up(value, unit):
    return -(-value // unit) * unit


def dot_nt(a, b):
    return lax.dot_general(a, b, (((1,), (1,)), ((), ())), preferred_element_type=f32)


def dot_nn(a, b):
    return lax.dot_general(a, b, (((1,), (0,)), ((), ())), preferred_element_type=f32)


def dot_wide(a, b):
    rows = a.shape[0]
    one = a.astype(bf16)
    rest = a - one.astype(f32)
    two = rest.astype(bf16)
    three = (rest - two.astype(f32)).astype(bf16)
    parts = dot_nn(jnp.concatenate([one, two, three], axis=0), b)
    return parts[:rows] + (parts[rows : 2 * rows] + parts[2 * rows :])


def pack_rank(value, packed):
    if not packed:
        return value
    half = value.shape[0] // 2
    return jnp.concatenate([value[:half], value[half:]], axis=1)


def unpack_rank(value, packed):
    if not packed:
        return value
    half = value.shape[1] // 2
    return jnp.concatenate([value[:, :half], value[:, half:]], axis=0)


def kernel(
    T,
    G,
    rows,
    steps,
    kv_heads,
    block,
    CW,
    packed,
    x_in,
    wq_in,
    wo_in,
    a_in,
    b_in,
    oa_in,
    ob_in,
    k_in,
    v_in,
    ck_in,
    cv_in,
    len_in,
    out,
    x_v,
    wq_v,
    wo_v,
    a_v,
    oa_v,
    k_v,
    v_v,
    ck_v,
    cv_v,
    len_s,
    at_all,
    b_all,
    u_all,
    r_all,
    oat_all,
    ob_all,
    q_all,
    o_send,
    o_recv,
    rr_all,
    sib_send,
    sib_recv,
    p_send,
    p_recv,
    local_sem,
    tp_send,
    tp_recv,
    g_send,
    g_recv,
    sib_ssem,
    sib_rsem,
    p_ssem,
    p_rsem,
):
    t = lax.axis_index("tp")
    g = lax.axis_index("group")
    R = rows * steps
    chips = T // 2
    core = lax.rem(t, 2)
    chip = lax.div(t, 2)
    sibling = t + 1 - 2 * core
    D = u_all.shape[2]
    gh = T // kv_heads
    scale = D ** (-0.5)

    def local(src, dst, index):
        copy = pltpu.make_async_copy(src, dst, local_sem.at[index])
        copy.start()
        return copy

    load_a = local(a_in, a_v, 0)
    load_oa = local(oa_in, oa_v, 1)
    load_x = local(x_in, x_v, 2)
    load_wq = local(wq_in, wq_v, 3)
    load_b = local(b_in, b_all.at[g, t], 4)
    load_ob = local(ob_in, ob_all.at[g], 5)
    load_k = local(k_in, k_v, 6)
    load_v = local(v_in, v_v, 7)
    load_ck = local(ck_in, ck_v, 8)
    load_cv = local(cv_in, cv_v, 9)
    load_len = local(len_in, len_s, 10)
    load_wo = local(wo_in, wo_v, 11)

    barrier = pltpu.get_barrier_semaphore()
    for d in range(1, T):
        pl.semaphore_signal(
            barrier, inc=1, device_id={"tp": lax.rem(t + d, T)}, device_id_type=MESH
        )
    for e in range(1, G):
        pl.semaphore_signal(
            barrier, inc=1, device_id={"group": lax.rem(g + e, G)}, device_id_type=MESH
        )

    eye = (
        lax.broadcasted_iota(jnp.int32, (RANK_TILE, RANK_TILE), 0)
        == lax.broadcasted_iota(jnp.int32, (RANK_TILE, RANK_TILE), 1)
    ).astype(f32).astype(bf16)
    load_a.wait()
    at_all[g] = dot_nt(eye, a_v[...]).astype(bf16)
    pl.semaphore_wait(barrier, T - 1 + G - 1)

    pending = []

    def over_group(phase, src, dst):
        for e in range(1, G):
            copy = pltpu.make_async_remote_copy(
                src_ref=src,
                dst_ref=dst,
                send_sem=g_send.at[phase, e],
                recv_sem=g_recv.at[phase, e],
                device_id={"group": lax.rem(g + e, G)},
                device_id_type=MESH,
            )
            copy.start()
            pending.append(copy)

    def from_group(phase, slots):
        for e in range(1, G):
            sender = lax.rem(g - e + G, G)
            pltpu.make_async_remote_copy(
                src_ref=slots.at[sender],
                dst_ref=slots.at[sender],
                send_sem=g_send.at[phase, e],
                recv_sem=g_recv.at[phase, e],
                device_id={"group": sender},
                device_id_type=MESH,
            ).wait_recv()

    def over_tp(phase, src, dst):
        for d in range(1, T):
            peer = lax.rem(t + d, T)
            copy = pltpu.make_async_remote_copy(
                src_ref=src(peer),
                dst_ref=dst,
                send_sem=tp_send.at[phase, d],
                recv_sem=tp_recv.at[phase, d],
                device_id={"tp": peer},
                device_id_type=MESH,
            )
            copy.start()
            pending.append(copy)

    def from_tp(phase, slots):
        for d in range(1, T):
            sender = lax.rem(t - d + T, T)
            pltpu.make_async_remote_copy(
                src_ref=slots.at[sender],
                dst_ref=slots.at[sender],
                send_sem=tp_send.at[phase, d],
                recv_sem=tp_recv.at[phase, d],
                device_id={"tp": sender},
                device_id_type=MESH,
            ).wait_recv()

    over_group(0, at_all.at[g], at_all.at[g])
    load_b.wait()
    over_tp(0, lambda peer: b_all.at[g, t], b_all.at[g, t])

    load_x.wait()
    load_wq.wait()
    u_all[t] = dot_nn(x_v[...], wq_v[...])
    over_tp(1, lambda peer: u_all.at[t], u_all.at[t])

    from_group(0, at_all)
    factor = at_all[...].reshape(G * RANK_TILE, CW)
    x_part = x_v[:, pl.ds(pl.multiple_of(t * CW, LANES), CW)]
    r_all[t] = pack_rank(dot_nt(x_part, factor), packed)
    over_tp(2, lambda peer: r_all.at[t], r_all.at[t])

    from_tp(0, b_all.at[g])
    over_group(1, b_all.at[g], b_all.at[g])

    load_oa.wait()
    oat_all[g] = dot_nt(eye, oa_v[...]).astype(bf16)
    load_ob.wait()
    over_group(2, oat_all.at[g], oat_all.at[g])
    over_group(3, ob_all.at[g], ob_all.at[g])

    load_k.wait()
    load_v.wait()
    load_len.wait()
    load_ck.wait()
    load_cv.wait()
    from_tp(1, u_all)
    from_tp(2, r_all)
    rank_inputs = unpack_rank(jnp.sum(r_all[...], axis=0), packed)
    from_group(1, b_all)
    up = jnp.concatenate(
        [
            jnp.concatenate([b_all[i, h] for h in range(T)], axis=1)
            for i in range(G)
        ],
        axis=0,
    )
    adapter = adapter_scale * dot_wide(rank_inputs, up)
    queries = []
    for h in range(T):
        one = (u_all[h] + adapter[:, h * D : (h + 1) * D]).astype(bf16)
        q_all[h] = one
        queries.append(one.astype(f32))

    position = t * block + lax.broadcasted_iota(jnp.int32, (gh * steps, block), 1)
    lane = lax.broadcasted_iota(jnp.int32, (gh * steps, LANES), 1)
    share = LANES // (2 * rows)
    for j in range(kv_heads):
        stat = jnp.zeros((gh * steps, LANES), f32)
        for i in range(rows):
            grouped = jnp.concatenate(
                [
                    queries[h][i * steps : (i + 1) * steps]
                    for h in range(j * gh, (j + 1) * gh)
                ],
                axis=0,
            ).astype(bf16)
            at = (i * kv_heads + j) * block
            scores = dot_nt(grouped, k_v[at : at + block]) * scale
            visible = position < len_s[i]
            peak = jnp.max(
                jnp.where(visible, scores, masked_score), axis=1, keepdims=True
            )
            weights = jnp.where(visible, jnp.exp(scores - peak), 0.0)
            total = jnp.sum(weights, axis=1, keepdims=True)
            outputs = dot_nn(weights.astype(bf16), v_v[at : at + block])
            o_send[j * gh : (j + 1) * gh, i * steps : (i + 1) * steps, :] = (
                outputs.reshape(gh, steps, D)
            )
            stat = jnp.where(
                lane >= 2 * i * share,
                jnp.where(lane >= (2 * i + 1) * share, total, peak),
                stat,
            )
        o_send[j * gh : (j + 1) * gh, R : R + steps, :] = stat.reshape(
            gh, steps, LANES
        )
    over_tp(3, lambda peer: o_send.at[peer], o_recv.at[t])
    o_recv[t] = o_send[t]

    mine = q_all[t]
    fresh_scores = dot_nt(mine, ck_v[...]) * scale
    row_of = lax.broadcasted_iota(jnp.int32, (R, R), 0)
    col_of = lax.broadcasted_iota(jnp.int32, (R, R), 1)
    causal = (lax.div(row_of, steps) == lax.div(col_of, steps)) & (row_of >= col_of)
    fresh_peak = jnp.max(
        jnp.where(causal, fresh_scores, masked_score), axis=1, keepdims=True
    )
    fresh_weights = jnp.where(causal, jnp.exp(fresh_scores - fresh_peak), 0.0)
    fresh_sum = jnp.sum(fresh_weights, axis=1, keepdims=True)
    fresh_out = dot_nn(fresh_weights.astype(bf16), cv_v[...])

    from_group(2, oat_all)
    from_group(3, ob_all)
    load_wo.wait()

    from_tp(3, o_recv)
    stats = o_recv[:, R : R + steps, :]
    peaks, sums, outs = [], [], []
    for i in range(rows):
        block_peak = stats[:, :, 2 * i * share : 2 * i * share + 1]
        block_sum = stats[:, :, (2 * i + 1) * share : (2 * i + 1) * share + 1]
        top = jnp.max(block_peak, axis=0)
        rescale = jnp.exp(block_peak - top[None])
        peaks.append(top)
        sums.append(jnp.sum(rescale * block_sum, axis=0))
        outs.append(
            jnp.sum(rescale * o_recv[:, i * steps : (i + 1) * steps, :], axis=0)
        )
    cache_peak = jnp.concatenate(peaks, axis=0)
    cache_sum = jnp.concatenate(sums, axis=0)
    cache_out = jnp.concatenate(outs, axis=0)
    joint = jnp.maximum(cache_peak, fresh_peak)
    left = jnp.exp(cache_peak - joint)
    right = jnp.exp(fresh_peak - joint)
    numer = cache_out * left + fresh_out * right
    denom = cache_sum * left + fresh_sum * right
    context = (numer / denom).astype(bf16)

    rr_all[t] = pack_rank(
        dot_nt(context, oat_all[...].reshape(G * RANK_TILE, D)), packed
    )

    def columns(device):
        return wo_v[:, pl.ds(pl.multiple_of(device * CW, LANES), CW)]

    order = list(range(1, chips)) + [0]
    to_sibling = {}
    for j in order:
        there = lax.rem(chip + j, chips)
        sib_send[j] = dot_nn(context, columns(2 * there + 1 - core))
        copy = pltpu.make_async_remote_copy(
            src_ref=sib_send.at[j],
            dst_ref=sib_recv.at[j],
            send_sem=sib_ssem.at[j],
            recv_sem=sib_rsem.at[j],
            device_id={"tp": sibling},
            device_id_type=MESH,
        )
        copy.start()
        to_sibling[j] = copy
    over_tp(4, lambda peer: rr_all.at[t], rr_all.at[t])
    for j in order:
        there = lax.rem(chip + j, chips)
        p_send[j] = dot_nn(context, columns(2 * there + core))
    across = {}
    for j in order:
        there = lax.rem(chip + j, chips)
        to_sibling[j].wait_recv()
        p_send[j] += sib_recv[j]
        if j:
            copy = pltpu.make_async_remote_copy(
                src_ref=p_send.at[j],
                dst_ref=p_recv.at[j],
                send_sem=p_ssem.at[j],
                recv_sem=p_rsem.at[j],
                device_id={"tp": 2 * there + core},
                device_id_type=MESH,
            )
            copy.start()
            across[j] = copy
    from_tp(4, rr_all)
    rank_outputs = unpack_rank(jnp.sum(rr_all[...], axis=0), packed)
    result = p_send[0] + adapter_scale * dot_wide(
        rank_outputs, ob_all[...].reshape(G * RANK_TILE, CW)
    )
    for j in range(1, chips):
        across[j].wait_recv()
        result += p_recv[j]
    out[...] = result.astype(out.dtype)

    for copy in pending:
        copy.wait_send()
    for j in order:
        to_sibling[j].wait_send()
        if j:
            across[j].wait_send()


def padded(value, axis, size):
    if value.shape[axis] == size:
        return value
    widths = [(0, 0)] * value.ndim
    widths[axis] = (0, size - value.shape[axis])
    return jnp.pad(value, widths)


def chunked(value, axis, count, size):
    shape = value.shape
    if shape[axis] == count * size:
        return value
    split = shape[:axis] + (count, shape[axis] // count) + shape[axis + 1 :]
    value = padded(value.reshape(split), axis + 1, size)
    return value.reshape(shape[:axis] + (count * size,) + shape[axis + 1 :])


def on_device(
    decoding_input,
    query_weight,
    output_weight,
    query_down_factor,
    query_up_factor,
    output_down_factor,
    output_up_factor,
    stored_keys,
    stored_values,
    current_keys,
    current_values,
    lengths,
):
    T = lax.axis_size("tp")
    G = lax.axis_size("group")
    rows, steps, width = decoding_input.shape
    kv_heads, block, D = stored_keys.shape[1:]
    assert query_weight.shape[1] == D and T % 2 == 0
    R = rows * steps
    chunk = width // T
    CW = rounded_up(chunk, LANES)
    rank = G * RANK_TILE
    packed = 2 * rank == LANES
    rank_shape = (R // 2, LANES) if packed else (R, rank)

    x = chunked(decoding_input.reshape(R, width), 1, T, CW)
    wq = chunked(query_weight, 0, T, CW)
    wo = chunked(output_weight, 1, T, CW)
    a = padded(padded(query_down_factor, 1, RANK_TILE), 0, CW)
    b = padded(query_up_factor, 0, RANK_TILE)
    oa = padded(output_down_factor, 1, RANK_TILE)
    ob = padded(padded(output_up_factor, 0, RANK_TILE), 1, CW)
    k = stored_keys.reshape(rows * kv_heads * block, D)
    v = stored_values.reshape(rows * kv_heads * block, D)
    if kv_heads > 1:
        shared = lax.axis_index("tp") // (T // kv_heads)
        current_keys = lax.dynamic_slice_in_dim(current_keys, shared, 1, 2)
        current_values = lax.dynamic_slice_in_dim(current_values, shared, 1, 2)
    ck = current_keys.reshape(R, D)
    cv = current_values.reshape(R, D)

    vmem = pltpu.VMEM
    dma = pltpu.SemaphoreType.DMA
    result = pl.pallas_call(
        functools.partial(kernel, T, G, rows, steps, kv_heads, block, CW, packed),
        out_shape=jax.ShapeDtypeStruct((R, CW), bf16),
        in_specs=[pl.BlockSpec(memory_space=pl.ANY)] * 12,
        out_specs=pl.BlockSpec(memory_space=pltpu.VMEM),
        scratch_shapes=[
            vmem(x.shape, bf16),
            vmem(wq.shape, bf16),
            vmem(wo.shape, bf16),
            vmem(a.shape, bf16),
            vmem(oa.shape, bf16),
            vmem(k.shape, bf16),
            vmem(v.shape, bf16),
            vmem(ck.shape, bf16),
            vmem(cv.shape, bf16),
            pltpu.SMEM(lengths.shape, jnp.int32),
            vmem((G, RANK_TILE, CW), bf16),
            vmem((G, T, RANK_TILE, D), bf16),
            vmem((T, R, D), f32),
            vmem((T,) + rank_shape, f32),
            vmem((G, RANK_TILE, D), bf16),
            vmem((G, RANK_TILE, CW), bf16),
            vmem((T, R, D), bf16),
            vmem((T, R + steps, D), f32),
            vmem((T, R + steps, D), f32),
            vmem((T,) + rank_shape, f32),
            vmem((T // 2, R, CW), f32),
            vmem((T // 2, R, CW), f32),
            vmem((T // 2, R, CW), f32),
            vmem((T // 2, R, CW), f32),
            dma((12,)),
            dma((5, T)),
            dma((5, T)),
            dma((4, G)),
            dma((4, G)),
            dma((T // 2,)),
            dma((T // 2,)),
            dma((T // 2,)),
            dma((T // 2,)),
        ],
        compiler_params=pltpu.CompilerParams(
            collective_id=0, has_side_effects=True, vmem_limit_bytes=32 * 2**20
        ),
        cost_estimate=pl.CostEstimate(
            flops=4 * R * width * D, bytes_accessed=4 * width * D, transcendentals=0
        ),
    )(x, wq, wo, a, b, oa, ob, k, v, ck, cv, lengths)
    return result[:, :chunk].reshape(rows, steps, chunk)


def solution(mesh):
    in_specs = (
        P("group", None, None),
        P(None, "tp"),
        P("tp", None),
        P("tp", "group"),
        P("group", "tp"),
        P("tp", "group"),
        P("group", "tp"),
        P("group", None, "tp", None),
        P("group", None, "tp", None),
        P("group", None, None, None),
        P("group", None, None, None),
        P("group"),
    )
    out_specs = P("group", None, "tp")
    return jax.shard_map(
        on_device, mesh=mesh, in_specs=in_specs, out_specs=out_specs, check_vma=False
    )
```

```python
import functools

import jax
import jax.numpy as jnp
from jax import lax
from jax.experimental import pallas as pl
from jax.experimental.pallas import tpu as pltpu
from jax.sharding import PartitionSpec as P

adapter_scale = 2.0
masked_score = -1e30
f32 = jnp.float32
bf16 = jnp.bfloat16
MESH = pl.DeviceIdType.MESH
RANK_TILE = 16
LANES = 128


def rounded_up(value, unit):
    return -(-value // unit) * unit


def dot_nt(a, b):
    return lax.dot_general(a, b, (((1,), (1,)), ((), ())), preferred_element_type=f32)


def dot_nn(a, b):
    return lax.dot_general(a, b, (((1,), (0,)), ((), ())), preferred_element_type=f32)


def dot_wide(a, b):
    rows = a.shape[0]
    one = a.astype(bf16)
    rest = a - one.astype(f32)
    two = rest.astype(bf16)
    three = (rest - two.astype(f32)).astype(bf16)
    parts = dot_nn(jnp.concatenate([one, two, three], axis=0), b)
    return parts[:rows] + (parts[rows : 2 * rows] + parts[2 * rows :])


def pack_rank(value, packed):
    if not packed:
        return value
    half = value.shape[0] // 2
    return jnp.concatenate([value[:half], value[half:]], axis=1)


def unpack_rank(value, packed):
    if not packed:
        return value
    half = value.shape[1] // 2
    return jnp.concatenate([value[:, :half], value[:, half:]], axis=0)


def kernel(
    T,
    G,
    rows,
    steps,
    kv_heads,
    block,
    CW,
    packed,
    x_in,
    wq_in,
    wo_in,
    a_in,
    b_in,
    oa_in,
    ob_in,
    k_in,
    v_in,
    ck_in,
    cv_in,
    len_in,
    out,
    x_v,
    wq_v,
    wo_v,
    k_v,
    v_v,
    ck_v,
    cv_v,
    len_s,
    at_all,
    b_all,
    u_all,
    r_all,
    oat_all,
    ob_all,
    q_all,
    o_send,
    o_recv,
    rr_all,
    sib_send,
    sib_recv,
    p_send,
    p_recv,
    local_sem,
    tp_send,
    tp_recv,
    g_send,
    g_recv,
    sib_ssem,
    sib_rsem,
    p_ssem,
    p_rsem,
):
    t = lax.axis_index("tp")
    g = lax.axis_index("group")
    R = rows * steps
    chips = T // 2
    core = lax.rem(t, 2)
    chip = lax.div(t, 2)
    sibling = t + 1 - 2 * core
    D = u_all.shape[2]
    gh = T // kv_heads
    scale = D ** (-0.5)

    def local(src, dst, index):
        copy = pltpu.make_async_copy(src, dst, local_sem.at[index])
        copy.start()
        return copy

    load_a = local(a_in, at_all.at[g], 0)
    load_oa = local(oa_in, oat_all.at[g], 1)
    load_x = local(x_in, x_v, 2)
    load_wq = local(wq_in, wq_v, 3)
    load_b = local(b_in, b_all.at[g, t], 4)
    load_ob = local(ob_in, ob_all.at[g], 5)
    load_k = local(k_in, k_v, 6)
    load_v = local(v_in, v_v, 7)
    load_ck = local(ck_in, ck_v, 8)
    load_cv = local(cv_in, cv_v, 9)
    load_len = local(len_in, len_s, 10)
    load_wo = local(wo_in, wo_v, 11)

    barrier = pltpu.get_barrier_semaphore()
    for d in range(1, T):
        pl.semaphore_signal(
            barrier, inc=1, device_id={"tp": lax.rem(t + d, T)}, device_id_type=MESH
        )
    for e in range(1, G):
        pl.semaphore_signal(
            barrier, inc=1, device_id={"group": lax.rem(g + e, G)}, device_id_type=MESH
        )

    load_a.wait()
    pl.semaphore_wait(barrier, T - 1 + G - 1)

    pending = []

    def over_group(phase, src, dst):
        for e in range(1, G):
            copy = pltpu.make_async_remote_copy(
                src_ref=src,
                dst_ref=dst,
                send_sem=g_send.at[phase, e],
                recv_sem=g_recv.at[phase, e],
                device_id={"group": lax.rem(g + e, G)},
                device_id_type=MESH,
            )
            copy.start()
            pending.append(copy)

    def from_group(phase, slots):
        for e in range(1, G):
            sender = lax.rem(g - e + G, G)
            pltpu.make_async_remote_copy(
                src_ref=slots.at[sender],
                dst_ref=slots.at[sender],
                send_sem=g_send.at[phase, e],
                recv_sem=g_recv.at[phase, e],
                device_id={"group": sender},
                device_id_type=MESH,
            ).wait_recv()

    def over_tp(phase, src, dst):
        for d in range(1, T):
            peer = lax.rem(t + d, T)
            copy = pltpu.make_async_remote_copy(
                src_ref=src(peer),
                dst_ref=dst,
                send_sem=tp_send.at[phase, d],
                recv_sem=tp_recv.at[phase, d],
                device_id={"tp": peer},
                device_id_type=MESH,
            )
            copy.start()
            pending.append(copy)

    def from_tp(phase, slots):
        for d in range(1, T):
            sender = lax.rem(t - d + T, T)
            pltpu.make_async_remote_copy(
                src_ref=slots.at[sender],
                dst_ref=slots.at[sender],
                send_sem=tp_send.at[phase, d],
                recv_sem=tp_recv.at[phase, d],
                device_id={"tp": sender},
                device_id_type=MESH,
            ).wait_recv()

    over_group(0, at_all.at[g], at_all.at[g])
    load_b.wait()
    over_tp(0, lambda peer: b_all.at[g, t], b_all.at[g, t])

    load_x.wait()
    load_wq.wait()
    u_all[t] = dot_nn(x_v[...], wq_v[...])
    over_tp(1, lambda peer: u_all.at[t], u_all.at[t])

    from_group(0, at_all)
    factor = at_all[...].reshape(G * RANK_TILE, CW)
    x_part = x_v[:, pl.ds(pl.multiple_of(t * CW, LANES), CW)]
    r_all[t] = pack_rank(dot_nt(x_part, factor), packed)
    over_tp(2, lambda peer: r_all.at[t], r_all.at[t])

    from_tp(0, b_all.at[g])
    over_group(1, b_all.at[g], b_all.at[g])

    load_oa.wait()
    load_ob.wait()
    over_group(2, oat_all.at[g], oat_all.at[g])
    over_group(3, ob_all.at[g], ob_all.at[g])

    load_k.wait()
    load_v.wait()
    load_len.wait()
    load_ck.wait()
    load_cv.wait()
    from_tp(1, u_all)
    from_tp(2, r_all)
    rank_inputs = unpack_rank(jnp.sum(r_all[...], axis=0), packed)
    from_group(1, b_all)
    up = jnp.concatenate(
        [
            jnp.concatenate([b_all[i, h] for h in range(T)], axis=1)
            for i in range(G)
        ],
        axis=0,
    )
    adapter = adapter_scale * dot_wide(rank_inputs, up)
    queries = []
    for h in range(T):
        one = (u_all[h] + adapter[:, h * D : (h + 1) * D]).astype(bf16)
        q_all[h] = one
        queries.append(one.astype(f32))

    position = t * block + lax.broadcasted_iota(jnp.int32, (gh * steps, block), 1)
    lane = lax.broadcasted_iota(jnp.int32, (gh * steps, LANES), 1)
    share = LANES // (2 * rows)
    for j in range(kv_heads):
        stat = jnp.zeros((gh * steps, LANES), f32)
        for i in range(rows):
            grouped = jnp.concatenate(
                [
                    queries[h][i * steps : (i + 1) * steps]
                    for h in range(j * gh, (j + 1) * gh)
                ],
                axis=0,
            ).astype(bf16)
            at = (i * kv_heads + j) * block
            scores = dot_nt(grouped, k_v[at : at + block]) * scale
            visible = position < len_s[i]
            peak = jnp.max(
                jnp.where(visible, scores, masked_score), axis=1, keepdims=True
            )
            weights = jnp.where(visible, jnp.exp(scores - peak), 0.0)
            total = jnp.sum(weights, axis=1, keepdims=True)
            outputs = dot_nn(weights.astype(bf16), v_v[at : at + block])
            o_send[j * gh : (j + 1) * gh, i * steps : (i + 1) * steps, :] = (
                outputs.reshape(gh, steps, D)
            )
            stat = jnp.where(
                lane >= 2 * i * share,
                jnp.where(lane >= (2 * i + 1) * share, total, peak),
                stat,
            )
        o_send[j * gh : (j + 1) * gh, R : R + steps, :] = stat.reshape(
            gh, steps, LANES
        )
    over_tp(3, lambda peer: o_send.at[peer], o_recv.at[t])
    o_recv[t] = o_send[t]

    mine = q_all[t]
    fresh_scores = dot_nt(mine, ck_v[...]) * scale
    row_of = lax.broadcasted_iota(jnp.int32, (R, R), 0)
    col_of = lax.broadcasted_iota(jnp.int32, (R, R), 1)
    causal = (lax.div(row_of, steps) == lax.div(col_of, steps)) & (row_of >= col_of)
    fresh_peak = jnp.max(
        jnp.where(causal, fresh_scores, masked_score), axis=1, keepdims=True
    )
    fresh_weights = jnp.where(causal, jnp.exp(fresh_scores - fresh_peak), 0.0)
    fresh_sum = jnp.sum(fresh_weights, axis=1, keepdims=True)
    fresh_out = dot_nn(fresh_weights.astype(bf16), cv_v[...])

    from_group(2, oat_all)
    from_group(3, ob_all)
    load_wo.wait()

    from_tp(3, o_recv)
    stats = o_recv[:, R : R + steps, :]
    peaks, sums, outs = [], [], []
    for i in range(rows):
        block_peak = stats[:, :, 2 * i * share : 2 * i * share + 1]
        block_sum = stats[:, :, (2 * i + 1) * share : (2 * i + 1) * share + 1]
        top = jnp.max(block_peak, axis=0)
        rescale = jnp.exp(block_peak - top[None])
        peaks.append(top)
        sums.append(jnp.sum(rescale * block_sum, axis=0))
        outs.append(
            jnp.sum(rescale * o_recv[:, i * steps : (i + 1) * steps, :], axis=0)
        )
    cache_peak = jnp.concatenate(peaks, axis=0)
    cache_sum = jnp.concatenate(sums, axis=0)
    cache_out = jnp.concatenate(outs, axis=0)
    joint = jnp.maximum(cache_peak, fresh_peak)
    left = jnp.exp(cache_peak - joint)
    right = jnp.exp(fresh_peak - joint)
    numer = cache_out * left + fresh_out * right
    denom = cache_sum * left + fresh_sum * right
    context = (numer / denom).astype(bf16)

    rr_all[t] = pack_rank(
        dot_nt(context, oat_all[...].reshape(G * RANK_TILE, D)), packed
    )

    def columns(device):
        return wo_v[:, pl.ds(pl.multiple_of(device * CW, LANES), CW)]

    order = list(range(1, chips)) + [0]
    to_sibling = {}
    for j in order:
        there = lax.rem(chip + j, chips)
        sib_send[j] = dot_nn(context, columns(2 * there + 1 - core))
        copy = pltpu.make_async_remote_copy(
            src_ref=sib_send.at[j],
            dst_ref=sib_recv.at[j],
            send_sem=sib_ssem.at[j],
            recv_sem=sib_rsem.at[j],
            device_id={"tp": sibling},
            device_id_type=MESH,
        )
        copy.start()
        to_sibling[j] = copy
    over_tp(4, lambda peer: rr_all.at[t], rr_all.at[t])
    for j in order:
        there = lax.rem(chip + j, chips)
        p_send[j] = dot_nn(context, columns(2 * there + core))
    across = {}
    for j in order:
        there = lax.rem(chip + j, chips)
        to_sibling[j].wait_recv()
        p_send[j] += sib_recv[j]
        if j:
            copy = pltpu.make_async_remote_copy(
                src_ref=p_send.at[j],
                dst_ref=p_recv.at[j],
                send_sem=p_ssem.at[j],
                recv_sem=p_rsem.at[j],
                device_id={"tp": 2 * there + core},
                device_id_type=MESH,
            )
            copy.start()
            across[j] = copy
    from_tp(4, rr_all)
    rank_outputs = unpack_rank(jnp.sum(rr_all[...], axis=0), packed)
    result = p_send[0] + adapter_scale * dot_wide(
        rank_outputs, ob_all[...].reshape(G * RANK_TILE, CW)
    )
    for j in range(1, chips):
        across[j].wait_recv()
        result += p_recv[j]
    out[...] = result.astype(out.dtype)

    for copy in pending:
        copy.wait_send()
    for j in order:
        to_sibling[j].wait_send()
        if j:
            across[j].wait_send()


def padded(value, axis, size):
    if value.shape[axis] == size:
        return value
    widths = [(0, 0)] * value.ndim
    widths[axis] = (0, size - value.shape[axis])
    return jnp.pad(value, widths)


def chunked(value, axis, count, size):
    shape = value.shape
    if shape[axis] == count * size:
        return value
    split = shape[:axis] + (count, shape[axis] // count) + shape[axis + 1 :]
    value = padded(value.reshape(split), axis + 1, size)
    return value.reshape(shape[:axis] + (count * size,) + shape[axis + 1 :])


def on_device(
    decoding_input,
    query_weight,
    output_weight,
    query_down_factor,
    query_up_factor,
    output_down_factor,
    output_up_factor,
    stored_keys,
    stored_values,
    current_keys,
    current_values,
    lengths,
):
    T = lax.axis_size("tp")
    G = lax.axis_size("group")
    rows, steps, width = decoding_input.shape
    kv_heads, block, D = stored_keys.shape[1:]
    assert query_weight.shape[1] == D and T % 2 == 0
    R = rows * steps
    chunk = width // T
    CW = rounded_up(chunk, LANES)
    rank = G * RANK_TILE
    packed = 2 * rank == LANES
    rank_shape = (R // 2, LANES) if packed else (R, rank)

    x = chunked(decoding_input.reshape(R, width), 1, T, CW)
    wq = chunked(query_weight, 0, T, CW)
    wo = chunked(output_weight, 1, T, CW)
    a = padded(padded(query_down_factor.T, 0, RANK_TILE), 1, CW)
    b = padded(query_up_factor, 0, RANK_TILE)
    oa = padded(output_down_factor.T, 0, RANK_TILE)
    ob = padded(padded(output_up_factor, 0, RANK_TILE), 1, CW)
    k = stored_keys.reshape(rows * kv_heads * block, D)
    v = stored_values.reshape(rows * kv_heads * block, D)
    if kv_heads > 1:
        shared = lax.axis_index("tp") // (T // kv_heads)
        current_keys = lax.dynamic_slice_in_dim(current_keys, shared, 1, 2)
        current_values = lax.dynamic_slice_in_dim(current_values, shared, 1, 2)
    ck = current_keys.reshape(R, D)
    cv = current_values.reshape(R, D)

    vmem = pltpu.VMEM
    dma = pltpu.SemaphoreType.DMA
    result = pl.pallas_call(
        functools.partial(kernel, T, G, rows, steps, kv_heads, block, CW, packed),
        out_shape=jax.ShapeDtypeStruct((R, CW), bf16),
        in_specs=[pl.BlockSpec(memory_space=pltpu.HBM)] * 12,
        out_specs=pl.BlockSpec(memory_space=pltpu.VMEM),
        scratch_shapes=[
            vmem(x.shape, bf16),
            vmem(wq.shape, bf16),
            vmem(wo.shape, bf16),
            vmem(k.shape, bf16),
            vmem(v.shape, bf16),
            vmem(ck.shape, bf16),
            vmem(cv.shape, bf16),
            pltpu.SMEM(lengths.shape, jnp.int32),
            vmem((G, RANK_TILE, CW), bf16),
            vmem((G, T, RANK_TILE, D), bf16),
            vmem((T, R, D), f32),
            vmem((T,) + rank_shape, f32),
            vmem((G, RANK_TILE, D), bf16),
            vmem((G, RANK_TILE, CW), bf16),
            vmem((T, R, D), bf16),
            vmem((T, R + steps, D), f32),
            vmem((T, R + steps, D), f32),
            vmem((T,) + rank_shape, f32),
            vmem((T // 2, R, CW), f32),
            vmem((T // 2, R, CW), f32),
            vmem((T // 2, R, CW), f32),
            vmem((T // 2, R, CW), f32),
            dma((12,)),
            dma((5, T)),
            dma((5, T)),
            dma((4, G)),
            dma((4, G)),
            dma((T // 2,)),
            dma((T // 2,)),
            dma((T // 2,)),
            dma((T // 2,)),
        ],
        compiler_params=pltpu.CompilerParams(
            collective_id=0, has_side_effects=True, vmem_limit_bytes=56 * 2**20
        ),
        cost_estimate=pl.CostEstimate(
            flops=4 * R * width * D, bytes_accessed=4 * width * D, transcendentals=0
        ),
    )(x, wq, wo, a, b, oa, ob, k, v, ck, cv, lengths)
    return result[:, :chunk].reshape(rows, steps, chunk)


def solution(mesh):
    in_specs = (
        P("group", None, None),
        P(None, "tp"),
        P("tp", None),
        P("tp", "group"),
        P("group", "tp"),
        P("tp", "group"),
        P("group", "tp"),
        P("group", None, "tp", None),
        P("group", None, "tp", None),
        P("group", None, None, None),
        P("group", None, None, None),
        P("group"),
    )
    out_specs = P("group", None, "tp")
    return jax.shard_map(
        on_device, mesh=mesh, in_specs=in_specs, out_specs=out_specs, check_vma=False
    )
```

```python
import functools

import jax
import jax.numpy as jnp
from jax import lax
from jax.experimental import pallas as pl
from jax.experimental.pallas import tpu as pltpu
from jax.sharding import PartitionSpec as P

adapter_scale = 2.0
masked_score = -1e30
f32 = jnp.float32
bf16 = jnp.bfloat16
MESH = pl.DeviceIdType.MESH
RANK_TILE = 16
LANES = 128


def rounded_up(value, unit):
    return -(-value // unit) * unit


def dot_nt(a, b):
    return lax.dot_general(a, b, (((1,), (1,)), ((), ())), preferred_element_type=f32)


def dot_nn(a, b):
    return lax.dot_general(a, b, (((1,), (0,)), ((), ())), preferred_element_type=f32)


def dot_wide(a, b):
    rows = a.shape[0]
    one = a.astype(bf16)
    rest = a - one.astype(f32)
    two = rest.astype(bf16)
    three = (rest - two.astype(f32)).astype(bf16)
    parts = dot_nn(jnp.concatenate([one, two, three], axis=0), b)
    return parts[:rows] + (parts[rows : 2 * rows] + parts[2 * rows :])


def partner(index, bits):
    result, unit = index, 1
    while unit <= bits:
        if bits & unit:
            result = result + unit * (1 - 2 * lax.rem(lax.div(index, unit), 2))
        unit *= 2
    return result


def pack_rank(value, packed):
    if not packed:
        return value
    half = value.shape[0] // 2
    return jnp.concatenate([value[:half], value[half:]], axis=1)


def unpack_rank(value, packed):
    if not packed:
        return value
    half = value.shape[1] // 2
    return jnp.concatenate([value[:, :half], value[:, half:]], axis=0)


def kernel(
    T,
    G,
    rows,
    steps,
    kv_heads,
    block,
    CW,
    packed,
    x_in,
    wq_in,
    wo_in,
    a_in,
    b_in,
    oa_in,
    ob_in,
    k_in,
    v_in,
    ck_in,
    cv_in,
    len_in,
    out,
    x_v,
    wq_v,
    wo_v,
    k_v,
    v_v,
    ck_v,
    cv_v,
    len_s,
    at_all,
    b_all,
    u_all,
    r_all,
    oat_all,
    ob_all,
    q_all,
    o_send,
    o_recv,
    rr_all,
    sib_send,
    sib_recv,
    p_send,
    p_recv,
    local_sem,
    tp_send,
    tp_recv,
    g_send,
    g_recv,
    sib_ssem,
    sib_rsem,
    p_ssem,
    p_rsem,
):
    t = lax.axis_index("tp")
    g = lax.axis_index("group")
    R = rows * steps
    chips = T // 2
    core = lax.rem(t, 2)
    chip = lax.div(t, 2)
    sibling = t + 1 - 2 * core
    D = u_all.shape[2]
    gh = T // kv_heads
    scale = D ** (-0.5)

    def local(src, dst, index):
        copy = pltpu.make_async_copy(src, dst, local_sem.at[index])
        copy.start()
        return copy

    load_a = local(a_in, at_all.at[g], 0)
    load_oa = local(oa_in, oat_all.at[g], 1)
    load_x = local(x_in, x_v, 2)
    load_wq = local(wq_in, wq_v, 3)
    load_b = local(b_in, b_all.at[g, t], 4)
    load_ob = local(ob_in, ob_all.at[g], 5)
    load_k = local(k_in, k_v, 6)
    load_v = local(v_in, v_v, 7)
    load_ck = local(ck_in, ck_v, 8)
    load_cv = local(cv_in, cv_v, 9)
    load_len = local(len_in, len_s, 10)
    load_wo = local(wo_in, wo_v, 11)

    barrier = pltpu.get_barrier_semaphore()
    for d in range(1, T):
        pl.semaphore_signal(
            barrier, inc=1, device_id={"tp": lax.rem(t + d, T)}, device_id_type=MESH
        )
    for e in range(1, G):
        pl.semaphore_signal(
            barrier, inc=1, device_id={"group": lax.rem(g + e, G)}, device_id_type=MESH
        )

    load_x.wait()
    load_wq.wait()
    u_all[t] = dot_nn(x_v[...], wq_v[...])
    load_a.wait()
    load_b.wait()
    pl.semaphore_wait(barrier, T - 1 + G - 1)

    pending = []

    def over_group(phase, src, dst):
        for e in range(1, G):
            copy = pltpu.make_async_remote_copy(
                src_ref=src,
                dst_ref=dst,
                send_sem=g_send.at[phase, e],
                recv_sem=g_recv.at[phase, e],
                device_id={"group": lax.rem(g + e, G)},
                device_id_type=MESH,
            )
            copy.start()
            pending.append(copy)

    def from_group(phase, slots):
        for e in range(1, G):
            sender = lax.rem(g - e + G, G)
            pltpu.make_async_remote_copy(
                src_ref=slots.at[sender],
                dst_ref=slots.at[sender],
                send_sem=g_send.at[phase, e],
                recv_sem=g_recv.at[phase, e],
                device_id={"group": sender},
                device_id_type=MESH,
            ).wait_recv()

    def over_tp(phase, src, dst):
        for d in reversed(range(1, T)):
            peer = partner(t, d)
            copy = pltpu.make_async_remote_copy(
                src_ref=src(peer),
                dst_ref=dst,
                send_sem=tp_send.at[phase, d],
                recv_sem=tp_recv.at[phase, d],
                device_id={"tp": peer},
                device_id_type=MESH,
            )
            copy.start()
            pending.append(copy)

    def from_tp(phase, slots):
        for d in range(1, T):
            sender = partner(t, d)
            pltpu.make_async_remote_copy(
                src_ref=slots.at[sender],
                dst_ref=slots.at[sender],
                send_sem=tp_send.at[phase, d],
                recv_sem=tp_recv.at[phase, d],
                device_id={"tp": sender},
                device_id_type=MESH,
            ).wait_recv()

    over_group(0, at_all.at[g], at_all.at[g])
    over_tp(0, lambda peer: b_all.at[g, t], b_all.at[g, t])

    over_tp(1, lambda peer: u_all.at[t], u_all.at[t])

    from_group(0, at_all)
    factor = at_all[...].reshape(G * RANK_TILE, CW)
    x_part = x_v[:, pl.ds(pl.multiple_of(t * CW, LANES), CW)]
    r_all[t] = pack_rank(dot_nt(x_part, factor), packed)
    over_tp(2, lambda peer: r_all.at[t], r_all.at[t])

    from_tp(0, b_all.at[g])
    over_group(1, b_all.at[g], b_all.at[g])

    load_k.wait()
    load_v.wait()
    load_len.wait()
    load_ck.wait()
    load_cv.wait()
    from_tp(1, u_all)
    from_tp(2, r_all)
    rank_inputs = unpack_rank(jnp.sum(r_all[...], axis=0), packed)
    from_group(1, b_all)
    up = jnp.concatenate(
        [
            jnp.concatenate([b_all[i, h] for h in range(T)], axis=1)
            for i in range(G)
        ],
        axis=0,
    )
    adapter = adapter_scale * dot_wide(rank_inputs, up)
    queries = []
    for h in range(T):
        one = (u_all[h] + adapter[:, h * D : (h + 1) * D]).astype(bf16)
        q_all[h] = one
        queries.append(one.astype(f32))

    position = t * block + lax.broadcasted_iota(jnp.int32, (gh * steps, block), 1)
    lane = lax.broadcasted_iota(jnp.int32, (gh * steps, LANES), 1)
    share = LANES // (2 * rows)
    for j in range(kv_heads):
        stat = jnp.zeros((gh * steps, LANES), f32)
        for i in range(rows):
            grouped = jnp.concatenate(
                [
                    queries[h][i * steps : (i + 1) * steps]
                    for h in range(j * gh, (j + 1) * gh)
                ],
                axis=0,
            ).astype(bf16)
            at = (i * kv_heads + j) * block
            scores = dot_nt(grouped, k_v[at : at + block]) * scale
            visible = position < len_s[i]
            peak = jnp.max(
                jnp.where(visible, scores, masked_score), axis=1, keepdims=True
            )
            weights = jnp.where(visible, jnp.exp(scores - peak), 0.0)
            total = jnp.sum(weights, axis=1, keepdims=True)
            outputs = dot_nn(weights.astype(bf16), v_v[at : at + block])
            o_send[j * gh : (j + 1) * gh, i * steps : (i + 1) * steps, :] = (
                outputs.reshape(gh, steps, D)
            )
            stat = jnp.where(
                lane >= 2 * i * share,
                jnp.where(lane >= (2 * i + 1) * share, total, peak),
                stat,
            )
        o_send[j * gh : (j + 1) * gh, R : R + steps, :] = stat.reshape(
            gh, steps, LANES
        )
    over_tp(3, lambda peer: o_send.at[peer], o_recv.at[t])
    o_recv[t] = o_send[t]
    load_oa.wait()
    load_ob.wait()
    over_group(2, oat_all.at[g], oat_all.at[g])
    over_group(3, ob_all.at[g], ob_all.at[g])

    mine = q_all[t]
    fresh_scores = dot_nt(mine, ck_v[...]) * scale
    row_of = lax.broadcasted_iota(jnp.int32, (R, R), 0)
    col_of = lax.broadcasted_iota(jnp.int32, (R, R), 1)
    causal = (lax.div(row_of, steps) == lax.div(col_of, steps)) & (row_of >= col_of)
    fresh_peak = jnp.max(
        jnp.where(causal, fresh_scores, masked_score), axis=1, keepdims=True
    )
    fresh_weights = jnp.where(causal, jnp.exp(fresh_scores - fresh_peak), 0.0)
    fresh_sum = jnp.sum(fresh_weights, axis=1, keepdims=True)
    fresh_out = dot_nn(fresh_weights.astype(bf16), cv_v[...])

    from_group(2, oat_all)
    from_group(3, ob_all)
    load_wo.wait()

    from_tp(3, o_recv)
    stats = o_recv[:, R : R + steps, :]
    peaks, sums, outs = [], [], []
    for i in range(rows):
        block_peak = stats[:, :, 2 * i * share : 2 * i * share + 1]
        block_sum = stats[:, :, (2 * i + 1) * share : (2 * i + 1) * share + 1]
        top = jnp.max(block_peak, axis=0)
        rescale = jnp.exp(block_peak - top[None])
        peaks.append(top)
        sums.append(jnp.sum(rescale * block_sum, axis=0))
        outs.append(
            jnp.sum(rescale * o_recv[:, i * steps : (i + 1) * steps, :], axis=0)
        )
    cache_peak = jnp.concatenate(peaks, axis=0)
    cache_sum = jnp.concatenate(sums, axis=0)
    cache_out = jnp.concatenate(outs, axis=0)
    joint = jnp.maximum(cache_peak, fresh_peak)
    left = jnp.exp(cache_peak - joint)
    right = jnp.exp(fresh_peak - joint)
    numer = cache_out * left + fresh_out * right
    denom = cache_sum * left + fresh_sum * right
    context = (numer / denom).astype(bf16)

    rr_all[t] = pack_rank(
        dot_nt(context, oat_all[...].reshape(G * RANK_TILE, D)), packed
    )

    def columns(device):
        return wo_v[:, pl.ds(pl.multiple_of(device * CW, LANES), CW)]

    order = list(reversed(range(chips)))
    to_sibling = {}
    for j in order:
        there = partner(chip, j)
        sib_send[j] = dot_nn(context, columns(2 * there + 1 - core))
        copy = pltpu.make_async_remote_copy(
            src_ref=sib_send.at[j],
            dst_ref=sib_recv.at[j],
            send_sem=sib_ssem.at[j],
            recv_sem=sib_rsem.at[j],
            device_id={"tp": sibling},
            device_id_type=MESH,
        )
        copy.start()
        to_sibling[j] = copy
    over_tp(4, lambda peer: rr_all.at[t], rr_all.at[t])
    for j in order:
        there = partner(chip, j)
        p_send[j] = dot_nn(context, columns(2 * there + core))
    across = {}
    for j in order:
        there = partner(chip, j)
        to_sibling[j].wait_recv()
        p_send[j] += sib_recv[j]
        if j:
            copy = pltpu.make_async_remote_copy(
                src_ref=p_send.at[j],
                dst_ref=p_recv.at[j],
                send_sem=p_ssem.at[j],
                recv_sem=p_rsem.at[j],
                device_id={"tp": 2 * there + core},
                device_id_type=MESH,
            )
            copy.start()
            across[j] = copy
    from_tp(4, rr_all)
    rank_outputs = unpack_rank(jnp.sum(rr_all[...], axis=0), packed)
    result = p_send[0] + adapter_scale * dot_wide(
        rank_outputs, ob_all[...].reshape(G * RANK_TILE, CW)
    )
    for j in range(1, chips):
        across[j].wait_recv()
        result += p_recv[j]
    out[...] = result.astype(out.dtype)

    for copy in pending:
        copy.wait_send()
    for j in order:
        to_sibling[j].wait_send()
        if j:
            across[j].wait_send()


def padded(value, axis, size):
    if value.shape[axis] == size:
        return value
    widths = [(0, 0)] * value.ndim
    widths[axis] = (0, size - value.shape[axis])
    return jnp.pad(value, widths)


def chunked(value, axis, count, size):
    shape = value.shape
    if shape[axis] == count * size:
        return value
    split = shape[:axis] + (count, shape[axis] // count) + shape[axis + 1 :]
    value = padded(value.reshape(split), axis + 1, size)
    return value.reshape(shape[:axis] + (count * size,) + shape[axis + 1 :])


def on_device(
    decoding_input,
    query_weight,
    output_weight,
    query_down_factor,
    query_up_factor,
    output_down_factor,
    output_up_factor,
    stored_keys,
    stored_values,
    current_keys,
    current_values,
    lengths,
):
    T = lax.axis_size("tp")
    G = lax.axis_size("group")
    rows, steps, width = decoding_input.shape
    kv_heads, block, D = stored_keys.shape[1:]
    assert query_weight.shape[1] == D and T > 1 and T & (T - 1) == 0
    R = rows * steps
    chunk = width // T
    CW = rounded_up(chunk, LANES)
    rank = G * RANK_TILE
    packed = 2 * rank == LANES
    rank_shape = (R // 2, LANES) if packed else (R, rank)

    x = chunked(decoding_input.reshape(R, width), 1, T, CW)
    wq = chunked(query_weight, 0, T, CW)
    wo = chunked(output_weight, 1, T, CW)
    a = padded(padded(query_down_factor.T, 0, RANK_TILE), 1, CW)
    b = padded(query_up_factor, 0, RANK_TILE)
    oa = padded(output_down_factor.T, 0, RANK_TILE)
    ob = padded(padded(output_up_factor, 0, RANK_TILE), 1, CW)
    k = stored_keys.reshape(rows * kv_heads * block, D)
    v = stored_values.reshape(rows * kv_heads * block, D)
    if kv_heads > 1:
        shared = lax.axis_index("tp") // (T // kv_heads)
        current_keys = lax.dynamic_slice_in_dim(current_keys, shared, 1, 2)
        current_values = lax.dynamic_slice_in_dim(current_values, shared, 1, 2)
    ck = current_keys.reshape(R, D)
    cv = current_values.reshape(R, D)

    vmem = pltpu.VMEM
    dma = pltpu.SemaphoreType.DMA
    result = pl.pallas_call(
        functools.partial(kernel, T, G, rows, steps, kv_heads, block, CW, packed),
        out_shape=jax.ShapeDtypeStruct((R, CW), bf16),
        in_specs=[pl.BlockSpec(memory_space=pltpu.HBM)] * 12,
        out_specs=pl.BlockSpec(memory_space=pltpu.VMEM),
        scratch_shapes=[
            vmem(x.shape, bf16),
            vmem(wq.shape, bf16),
            vmem(wo.shape, bf16),
            vmem(k.shape, bf16),
            vmem(v.shape, bf16),
            vmem(ck.shape, bf16),
            vmem(cv.shape, bf16),
            pltpu.SMEM(lengths.shape, jnp.int32),
            vmem((G, RANK_TILE, CW), bf16),
            vmem((G, T, RANK_TILE, D), bf16),
            vmem((T, R, D), f32),
            vmem((T,) + rank_shape, f32),
            vmem((G, RANK_TILE, D), bf16),
            vmem((G, RANK_TILE, CW), bf16),
            vmem((T, R, D), bf16),
            vmem((T, R + steps, D), f32),
            vmem((T, R + steps, D), f32),
            vmem((T,) + rank_shape, f32),
            vmem((T // 2, R, CW), f32),
            vmem((T // 2, R, CW), f32),
            vmem((T // 2, R, CW), f32),
            vmem((T // 2, R, CW), f32),
            dma((12,)),
            dma((5, T)),
            dma((5, T)),
            dma((4, G)),
            dma((4, G)),
            dma((T // 2,)),
            dma((T // 2,)),
            dma((T // 2,)),
            dma((T // 2,)),
        ],
        compiler_params=pltpu.CompilerParams(
            collective_id=0, has_side_effects=True, vmem_limit_bytes=56 * 2**20
        ),
        cost_estimate=pl.CostEstimate(
            flops=4 * R * width * D, bytes_accessed=4 * width * D, transcendentals=0
        ),
    )(x, wq, wo, a, b, oa, ob, k, v, ck, cv, lengths)
    return result[:, :chunk].reshape(rows, steps, chunk)


def solution(mesh):
    in_specs = (
        P("group", None, None),
        P(None, "tp"),
        P("tp", None),
        P("tp", "group"),
        P("group", "tp"),
        P("tp", "group"),
        P("group", "tp"),
        P("group", None, "tp", None),
        P("group", None, "tp", None),
        P("group", None, None, None),
        P("group", None, None, None),
        P("group"),
    )
    out_specs = P("group", None, "tp")
    return jax.shard_map(
        on_device, mesh=mesh, in_specs=in_specs, out_specs=out_specs, check_vma=False
    )
```

```python
import functools

import jax
import jax.numpy as jnp
from jax import lax
from jax.experimental import pallas as pl
from jax.experimental.pallas import tpu as pltpu
from jax.sharding import PartitionSpec as P

adapter_scale = 2.0
masked_score = -1e30
f32 = jnp.float32
bf16 = jnp.bfloat16
MESH = pl.DeviceIdType.MESH
RANK_TILE = 16
LANES = 128


def rounded_up(value, unit):
    return -(-value // unit) * unit


def dot_nt(a, b):
    return lax.dot_general(a, b, (((1,), (1,)), ((), ())), preferred_element_type=f32)


def dot_nn(a, b):
    return lax.dot_general(a, b, (((1,), (0,)), ((), ())), preferred_element_type=f32)


def dot_wide(a, b):
    rows = a.shape[0]
    one = a.astype(bf16)
    rest = a - one.astype(f32)
    two = rest.astype(bf16)
    three = (rest - two.astype(f32)).astype(bf16)
    parts = dot_nn(jnp.concatenate([one, two, three], axis=0), b)
    return parts[:rows] + (parts[rows : 2 * rows] + parts[2 * rows :])


def partner(index, bits):
    result, unit = index, 1
    while unit <= bits:
        if bits & unit:
            result = result + unit * (1 - 2 * lax.rem(lax.div(index, unit), 2))
        unit *= 2
    return result


def pack_rank(value, packed):
    if not packed:
        return value
    half = value.shape[0] // 2
    return jnp.concatenate([value[:half], value[half:]], axis=1)


def unpack_rank(value, packed):
    if not packed:
        return value
    half = value.shape[1] // 2
    return jnp.concatenate([value[:, :half], value[:, half:]], axis=0)


def kernel(
    T,
    G,
    rows,
    steps,
    kv_heads,
    block,
    CW,
    packed,
    x_in,
    wq_in,
    wo_in,
    a_in,
    b_in,
    oa_in,
    ob_in,
    k_in,
    v_in,
    ck_in,
    cv_in,
    len_in,
    out,
    x_v,
    wq_v,
    wo_pair,
    k_v,
    v_v,
    ck_v,
    cv_v,
    len_s,
    at_all,
    b_all,
    u_all,
    r_all,
    oat_pair,
    ob_all,
    q_all,
    o_send,
    o_recv,
    rr_own,
    rr_recv,
    ctx_pair,
    p_send,
    p_recv,
    local_sem,
    tp_send,
    tp_recv,
    g_send,
    g_recv,
    sib_ssem,
    sib_rsem,
    p_ssem,
    p_rsem,
):
    t = lax.axis_index("tp")
    g = lax.axis_index("group")
    R = rows * steps
    chips = T // 2
    core = lax.rem(t, 2)
    chip = lax.div(t, 2)
    sibling = t + 1 - 2 * core
    D = u_all.shape[2]
    gh = T // kv_heads
    scale = D ** (-0.5)

    def local(src, dst, index):
        copy = pltpu.make_async_copy(src, dst, local_sem.at[index])
        copy.start()
        return copy

    load_a = local(a_in, at_all.at[g], 0)
    load_oa = local(oa_in, oat_pair.at[core, g], 1)
    load_x = local(x_in, x_v, 2)
    load_wq = local(wq_in, wq_v, 3)
    load_b = local(b_in, b_all.at[g, t], 4)
    load_ob = local(ob_in, ob_all.at[g], 5)
    load_k = local(k_in, k_v, 6)
    load_v = local(v_in, v_v, 7)
    load_ck = local(ck_in, ck_v, 8)
    load_cv = local(cv_in, cv_v, 9)
    load_len = local(len_in, len_s, 10)

    def columns(device):
        return wo_in.at[:, pl.ds(pl.multiple_of(device * CW, LANES), CW)]

    load_wo = [
        local(columns(2 * z + core), wo_pair.at[z, core], 11 + z) for z in range(chips)
    ]

    barrier = pltpu.get_barrier_semaphore()
    for d in range(1, T):
        pl.semaphore_signal(
            barrier, inc=1, device_id={"tp": lax.rem(t + d, T)}, device_id_type=MESH
        )
    for e in range(1, G):
        pl.semaphore_signal(
            barrier, inc=1, device_id={"group": lax.rem(g + e, G)}, device_id_type=MESH
        )

    load_x.wait()
    load_wq.wait()
    u_all[t] = dot_nn(x_v[...], wq_v[...])
    load_a.wait()
    load_b.wait()
    pl.semaphore_wait(barrier, T - 1 + G - 1)

    pending = []

    def over_group(phase, src, dst):
        for e in range(1, G):
            copy = pltpu.make_async_remote_copy(
                src_ref=src,
                dst_ref=dst,
                send_sem=g_send.at[phase, e],
                recv_sem=g_recv.at[phase, e],
                device_id={"group": lax.rem(g + e, G)},
                device_id_type=MESH,
            )
            copy.start()
            pending.append(copy)

    def from_group(phase, slots):
        for e in range(1, G):
            sender = lax.rem(g - e + G, G)
            pltpu.make_async_remote_copy(
                src_ref=slots.at[sender],
                dst_ref=slots.at[sender],
                send_sem=g_send.at[phase, e],
                recv_sem=g_recv.at[phase, e],
                device_id={"group": sender},
                device_id_type=MESH,
            ).wait_recv()

    def over_tp(phase, src, dst):
        for d in reversed(range(1, T)):
            peer = partner(t, d)
            copy = pltpu.make_async_remote_copy(
                src_ref=src(peer),
                dst_ref=dst,
                send_sem=tp_send.at[phase, d],
                recv_sem=tp_recv.at[phase, d],
                device_id={"tp": peer},
                device_id_type=MESH,
            )
            copy.start()
            pending.append(copy)

    def from_tp(phase, slots):
        for d in range(1, T):
            sender = partner(t, d)
            pltpu.make_async_remote_copy(
                src_ref=slots.at[sender],
                dst_ref=slots.at[sender],
                send_sem=tp_send.at[phase, d],
                recv_sem=tp_recv.at[phase, d],
                device_id={"tp": sender},
                device_id_type=MESH,
            ).wait_recv()

    over_group(0, at_all.at[g], at_all.at[g])
    over_tp(0, lambda peer: b_all.at[g, t], b_all.at[g, t])

    over_tp(1, lambda peer: u_all.at[t], u_all.at[t])

    from_group(0, at_all)
    factor = at_all[...].reshape(G * RANK_TILE, CW)
    x_part = x_v[:, pl.ds(pl.multiple_of(t * CW, LANES), CW)]
    r_all[t] = pack_rank(dot_nt(x_part, factor), packed)
    over_tp(2, lambda peer: r_all.at[t], r_all.at[t])

    from_tp(0, b_all.at[g])
    over_group(1, b_all.at[g], b_all.at[g])

    def to_sibling(index, src, dst):
        copy = pltpu.make_async_remote_copy(
            src_ref=src,
            dst_ref=dst,
            send_sem=sib_ssem.at[index],
            recv_sem=sib_rsem.at[index],
            device_id={"tp": sibling},
            device_id_type=MESH,
        )
        copy.start()
        pending.append(copy)

    def from_sibling(index, slot):
        pltpu.make_async_remote_copy(
            src_ref=slot,
            dst_ref=slot,
            send_sem=sib_ssem.at[index],
            recv_sem=sib_rsem.at[index],
            device_id={"tp": sibling},
            device_id_type=MESH,
        ).wait_recv()

    for z in range(chips):
        to_sibling(z, columns(2 * z + 1 - core), wo_pair.at[z, core])

    load_k.wait()
    load_v.wait()
    load_len.wait()
    load_ck.wait()
    load_cv.wait()
    from_tp(1, u_all)
    from_tp(2, r_all)
    rank_inputs = unpack_rank(jnp.sum(r_all[...], axis=0), packed)
    from_group(1, b_all)
    up = jnp.concatenate(
        [
            jnp.concatenate([b_all[i, h] for h in range(T)], axis=1)
            for i in range(G)
        ],
        axis=0,
    )
    adapter = adapter_scale * dot_wide(rank_inputs, up)
    queries = []
    for h in range(T):
        one = (u_all[h] + adapter[:, h * D : (h + 1) * D]).astype(bf16)
        q_all[h] = one
        queries.append(one.astype(f32))

    position = t * block + lax.broadcasted_iota(jnp.int32, (gh * steps, block), 1)
    lane = lax.broadcasted_iota(jnp.int32, (gh * steps, LANES), 1)
    share = LANES // (2 * rows)
    for j in range(kv_heads):
        stat = jnp.zeros((gh * steps, LANES), f32)
        for i in range(rows):
            grouped = jnp.concatenate(
                [
                    queries[h][i * steps : (i + 1) * steps]
                    for h in range(j * gh, (j + 1) * gh)
                ],
                axis=0,
            ).astype(bf16)
            at = (i * kv_heads + j) * block
            scores = dot_nt(grouped, k_v[at : at + block]) * scale
            visible = position < len_s[i]
            peak = jnp.max(
                jnp.where(visible, scores, masked_score), axis=1, keepdims=True
            )
            weights = jnp.where(visible, jnp.exp(scores - peak), 0.0)
            total = jnp.sum(weights, axis=1, keepdims=True)
            outputs = dot_nn(weights.astype(bf16), v_v[at : at + block])
            o_send[j * gh : (j + 1) * gh, i * steps : (i + 1) * steps, :] = (
                outputs.reshape(gh, steps, D)
            )
            stat = jnp.where(
                lane >= 2 * i * share,
                jnp.where(lane >= (2 * i + 1) * share, total, peak),
                stat,
            )
        o_send[j * gh : (j + 1) * gh, R : R + steps, :] = stat.reshape(
            gh, steps, LANES
        )
    over_tp(3, lambda peer: o_send.at[peer], o_recv.at[t])
    o_recv[t] = o_send[t]
    load_oa.wait()
    load_ob.wait()
    over_group(2, oat_pair.at[core, g], oat_pair.at[core, g])
    over_group(3, ob_all.at[g], ob_all.at[g])

    mine = q_all[t]
    fresh_scores = dot_nt(mine, ck_v[...]) * scale
    row_of = lax.broadcasted_iota(jnp.int32, (R, R), 0)
    col_of = lax.broadcasted_iota(jnp.int32, (R, R), 1)
    causal = (lax.div(row_of, steps) == lax.div(col_of, steps)) & (row_of >= col_of)
    fresh_peak = jnp.max(
        jnp.where(causal, fresh_scores, masked_score), axis=1, keepdims=True
    )
    fresh_weights = jnp.where(causal, jnp.exp(fresh_scores - fresh_peak), 0.0)
    fresh_sum = jnp.sum(fresh_weights, axis=1, keepdims=True)
    fresh_out = dot_nn(fresh_weights.astype(bf16), cv_v[...])

    from_group(2, oat_pair.at[core])
    to_sibling(chips, oat_pair.at[core], oat_pair.at[core])
    from_group(3, ob_all)
    for z in range(chips):
        load_wo[z].wait()
        from_sibling(z, wo_pair.at[z, 1 - core])
    from_sibling(chips, oat_pair.at[1 - core])

    from_tp(3, o_recv)
    stats = o_recv[:, R : R + steps, :]
    peaks, sums, outs = [], [], []
    for i in range(rows):
        block_peak = stats[:, :, 2 * i * share : 2 * i * share + 1]
        block_sum = stats[:, :, (2 * i + 1) * share : (2 * i + 1) * share + 1]
        top = jnp.max(block_peak, axis=0)
        rescale = jnp.exp(block_peak - top[None])
        peaks.append(top)
        sums.append(jnp.sum(rescale * block_sum, axis=0))
        outs.append(
            jnp.sum(rescale * o_recv[:, i * steps : (i + 1) * steps, :], axis=0)
        )
    cache_peak = jnp.concatenate(peaks, axis=0)
    cache_sum = jnp.concatenate(sums, axis=0)
    cache_out = jnp.concatenate(outs, axis=0)
    joint = jnp.maximum(cache_peak, fresh_peak)
    left = jnp.exp(cache_peak - joint)
    right = jnp.exp(fresh_peak - joint)
    numer = cache_out * left + fresh_out * right
    denom = cache_sum * left + fresh_sum * right
    ctx_pair[core] = (numer / denom).astype(bf16)

    to_sibling(chips + 1, ctx_pair.at[core], ctx_pair.at[core])
    from_sibling(chips + 1, ctx_pair.at[1 - core])
    context = jnp.concatenate([ctx_pair[0], ctx_pair[1]], axis=1)

    def across(index, j, src, dst):
        copy = pltpu.make_async_remote_copy(
            src_ref=src,
            dst_ref=dst,
            send_sem=p_ssem.at[index, j],
            recv_sem=p_rsem.at[index, j],
            device_id={"tp": 2 * partner(chip, j) + core},
            device_id_type=MESH,
        )
        copy.start()
        pending.append(copy)
        return copy

    arrivals = {}
    for j in reversed(range(chips)):
        p_send[j] = dot_nn(context, wo_pair[partner(chip, j)].reshape(2 * D, CW))
        if j:
            arrivals[j] = across(0, j, p_send.at[j], p_recv.at[j])
    rr_own[...] = pack_rank(
        dot_nt(ctx_pair[0], oat_pair[0].reshape(G * RANK_TILE, D))
        + dot_nt(ctx_pair[1], oat_pair[1].reshape(G * RANK_TILE, D)),
        packed,
    )
    ranks = {}
    for j in reversed(range(1, chips)):
        ranks[j] = across(1, j, rr_own, rr_recv.at[j])
    rank_sum = rr_own[...]
    for j in range(1, chips):
        ranks[j].wait_recv()
        rank_sum += rr_recv[j]
    rank_outputs = unpack_rank(rank_sum, packed)
    result = p_send[0] + adapter_scale * dot_wide(
        rank_outputs, ob_all[...].reshape(G * RANK_TILE, CW)
    )
    for j in range(1, chips):
        arrivals[j].wait_recv()
        result += p_recv[j]
    out[...] = result.astype(out.dtype)

    for copy in pending:
        copy.wait_send()


def padded(value, axis, size):
    if value.shape[axis] == size:
        return value
    widths = [(0, 0)] * value.ndim
    widths[axis] = (0, size - value.shape[axis])
    return jnp.pad(value, widths)


def chunked(value, axis, count, size):
    shape = value.shape
    if shape[axis] == count * size:
        return value
    split = shape[:axis] + (count, shape[axis] // count) + shape[axis + 1 :]
    value = padded(value.reshape(split), axis + 1, size)
    return value.reshape(shape[:axis] + (count * size,) + shape[axis + 1 :])


def on_device(
    decoding_input,
    query_weight,
    output_weight,
    query_down_factor,
    query_up_factor,
    output_down_factor,
    output_up_factor,
    stored_keys,
    stored_values,
    current_keys,
    current_values,
    lengths,
):
    T = lax.axis_size("tp")
    G = lax.axis_size("group")
    rows, steps, width = decoding_input.shape
    kv_heads, block, D = stored_keys.shape[1:]
    assert query_weight.shape[1] == D and T > 1 and T & (T - 1) == 0
    R = rows * steps
    chunk = width // T
    CW = rounded_up(chunk, LANES)
    rank = G * RANK_TILE
    packed = 2 * rank == LANES
    rank_shape = (R // 2, LANES) if packed else (R, rank)

    x = chunked(decoding_input.reshape(R, width), 1, T, CW)
    wq = chunked(query_weight, 0, T, CW)
    wo = chunked(output_weight, 1, T, CW)
    a = padded(padded(query_down_factor.T, 0, RANK_TILE), 1, CW)
    b = padded(query_up_factor, 0, RANK_TILE)
    oa = padded(output_down_factor.T, 0, RANK_TILE)
    ob = padded(padded(output_up_factor, 0, RANK_TILE), 1, CW)
    k = stored_keys.reshape(rows * kv_heads * block, D)
    v = stored_values.reshape(rows * kv_heads * block, D)
    if kv_heads > 1:
        shared = lax.axis_index("tp") // (T // kv_heads)
        current_keys = lax.dynamic_slice_in_dim(current_keys, shared, 1, 2)
        current_values = lax.dynamic_slice_in_dim(current_values, shared, 1, 2)
    ck = current_keys.reshape(R, D)
    cv = current_values.reshape(R, D)

    vmem = pltpu.VMEM
    dma = pltpu.SemaphoreType.DMA
    result = pl.pallas_call(
        functools.partial(kernel, T, G, rows, steps, kv_heads, block, CW, packed),
        out_shape=pltpu.VMEM((R, CW), bf16),
        in_specs=[pl.BlockSpec(memory_space=pltpu.HBM)] * 12,
        out_specs=pl.BlockSpec(memory_space=pltpu.VMEM),
        scratch_shapes=[
            vmem(x.shape, bf16),
            vmem(wq.shape, bf16),
            vmem((T // 2, 2, D, CW), bf16),
            vmem(k.shape, bf16),
            vmem(v.shape, bf16),
            vmem(ck.shape, bf16),
            vmem(cv.shape, bf16),
            pltpu.SMEM(lengths.shape, jnp.int32),
            vmem((G, RANK_TILE, CW), bf16),
            vmem((G, T, RANK_TILE, D), bf16),
            vmem((T, R, D), f32),
            vmem((T,) + rank_shape, f32),
            vmem((2, G, RANK_TILE, D), bf16),
            vmem((G, RANK_TILE, CW), bf16),
            vmem((T, R, D), bf16),
            vmem((T, R + steps, D), f32),
            vmem((T, R + steps, D), f32),
            vmem(rank_shape, f32),
            vmem((T // 2,) + rank_shape, f32),
            vmem((2, R, D), bf16),
            vmem((T // 2, R, CW), f32),
            vmem((T // 2, R, CW), f32),
            dma((11 + T // 2,)),
            dma((4, T)),
            dma((4, T)),
            dma((4, G)),
            dma((4, G)),
            dma((T // 2 + 2,)),
            dma((T // 2 + 2,)),
            dma((2, T // 2)),
            dma((2, T // 2)),
        ],
        compiler_params=pltpu.CompilerParams(
            collective_id=0, has_side_effects=True, vmem_limit_bytes=56 * 2**20
        ),
        cost_estimate=pl.CostEstimate(
            flops=4 * R * width * D, bytes_accessed=4 * width * D, transcendentals=0
        ),
    )(x, wq, wo, a, b, oa, ob, k, v, ck, cv, lengths)
    return result[:, :chunk].reshape(rows, steps, chunk)


def solution(mesh):
    in_specs = (
        P("group", None, None),
        P(None, "tp"),
        P("tp", None),
        P("tp", "group"),
        P("group", "tp"),
        P("tp", "group"),
        P("group", "tp"),
        P("group", None, "tp", None),
        P("group", None, "tp", None),
        P("group", None, None, None),
        P("group", None, None, None),
        P("group"),
    )
    out_specs = P("group", None, "tp")
    return jax.shard_map(
        on_device, mesh=mesh, in_specs=in_specs, out_specs=out_specs, check_vma=False
    )
```

```python
import functools

import jax
import jax.numpy as jnp
from jax import lax
from jax.experimental import pallas as pl
from jax.experimental.pallas import tpu as pltpu
from jax.sharding import PartitionSpec as P

adapter_scale = 2.0
masked_score = -1e30
f32 = jnp.float32
bf16 = jnp.bfloat16
MESH = pl.DeviceIdType.MESH
RANK_TILE = 16
LANES = 128


def rounded_up(value, unit):
    return -(-value // unit) * unit


def dot_nt(a, b):
    return lax.dot_general(a, b, (((1,), (1,)), ((), ())), preferred_element_type=f32)


def dot_nn(a, b):
    return lax.dot_general(a, b, (((1,), (0,)), ((), ())), preferred_element_type=f32)


def dot_wide(a, b):
    rows = a.shape[0]
    one = a.astype(bf16)
    rest = a - one.astype(f32)
    two = rest.astype(bf16)
    three = (rest - two.astype(f32)).astype(bf16)
    parts = dot_nn(jnp.concatenate([one, two, three], axis=0), b)
    return parts[:rows] + (parts[rows : 2 * rows] + parts[2 * rows :])


def partner(index, bits):
    result, unit = index, 1
    while unit <= bits:
        if bits & unit:
            result = result + unit * (1 - 2 * lax.rem(lax.div(index, unit), 2))
        unit *= 2
    return result


def pack_rank(value, packed):
    if not packed:
        return value
    half = value.shape[0] // 2
    return jnp.concatenate([value[:half], value[half:]], axis=1)


def unpack_rank(value, packed):
    if not packed:
        return value
    half = value.shape[1] // 2
    return jnp.concatenate([value[:, :half], value[:, half:]], axis=0)


def kernel(
    T,
    G,
    rows,
    steps,
    kv_heads,
    block,
    CW,
    packed,
    x_in,
    wq_in,
    wo_in,
    a_in,
    b_in,
    oa_in,
    ob_in,
    k_in,
    v_in,
    ck_in,
    cv_in,
    len_in,
    out,
    x_v,
    wq_v,
    wo_pair,
    k_v,
    v_v,
    ck_v,
    cv_v,
    len_s,
    at_all,
    b_all,
    u_all,
    r_all,
    oat_pair,
    ob_all,
    q_all,
    o_send,
    o_recv,
    rr_own,
    rr_recv,
    ctx_pair,
    p_send,
    p_recv,
    local_sem,
    tp_send,
    tp_recv,
    g_send,
    g_recv,
    sib_ssem,
    sib_rsem,
    p_ssem,
    p_rsem,
):
    t = lax.axis_index("tp")
    g = lax.axis_index("group")
    R = rows * steps
    chips = T // 2
    core = lax.rem(t, 2)
    chip = lax.div(t, 2)
    sibling = t + 1 - 2 * core
    D = u_all.shape[2]
    gh = T // kv_heads
    scale = D ** (-0.5)

    def local(src, dst, index):
        copy = pltpu.make_async_copy(src, dst, local_sem.at[index])
        copy.start()
        return copy

    load_a = local(a_in, at_all.at[g], 0)
    load_oa = local(oa_in, oat_pair.at[core, g], 1)
    load_x = local(x_in, x_v, 2)
    load_wq = local(wq_in, wq_v, 3)
    load_b = local(b_in, b_all.at[g, t], 4)
    load_ob = local(ob_in, ob_all.at[g], 5)
    load_k = local(k_in, k_v, 6)
    load_v = local(v_in, v_v, 7)
    load_ck = local(ck_in, ck_v, 8)
    load_cv = local(cv_in, cv_v, 9)
    load_len = local(len_in, len_s, 10)

    def columns(device):
        return wo_in.at[:, pl.ds(pl.multiple_of(device * CW, LANES), CW)]

    load_wo = [
        local(columns(2 * z + core), wo_pair.at[z, core], 11 + z) for z in range(chips)
    ]

    barrier = pltpu.get_barrier_semaphore()
    for d in range(1, T):
        pl.semaphore_signal(
            barrier, inc=1, device_id={"tp": lax.rem(t + d, T)}, device_id_type=MESH
        )
    for e in range(1, G):
        pl.semaphore_signal(
            barrier, inc=1, device_id={"group": lax.rem(g + e, G)}, device_id_type=MESH
        )

    load_x.wait()
    load_wq.wait()
    u_all[t] = dot_nn(x_v[...], wq_v[...])
    load_a.wait()
    load_b.wait()
    pl.semaphore_wait(barrier, T - 1 + G - 1)

    pending = []

    def over_group(phase, src, dst):
        for e in range(1, G):
            copy = pltpu.make_async_remote_copy(
                src_ref=src,
                dst_ref=dst,
                send_sem=g_send.at[phase, e],
                recv_sem=g_recv.at[phase, e],
                device_id={"group": lax.rem(g + e, G)},
                device_id_type=MESH,
            )
            copy.start()
            pending.append(copy)

    def from_group(phase, slots):
        for e in range(1, G):
            sender = lax.rem(g - e + G, G)
            pltpu.make_async_remote_copy(
                src_ref=slots.at[sender],
                dst_ref=slots.at[sender],
                send_sem=g_send.at[phase, e],
                recv_sem=g_recv.at[phase, e],
                device_id={"group": sender},
                device_id_type=MESH,
            ).wait_recv()

    def over_tp(phase, src, dst):
        for d in reversed(range(1, T)):
            peer = partner(t, d)
            copy = pltpu.make_async_remote_copy(
                src_ref=src(peer),
                dst_ref=dst,
                send_sem=tp_send.at[phase, d],
                recv_sem=tp_recv.at[phase, d],
                device_id={"tp": peer},
                device_id_type=MESH,
            )
            copy.start()
            pending.append(copy)

    def from_tp(phase, slots):
        for d in range(1, T):
            sender = partner(t, d)
            pltpu.make_async_remote_copy(
                src_ref=slots.at[sender],
                dst_ref=slots.at[sender],
                send_sem=tp_send.at[phase, d],
                recv_sem=tp_recv.at[phase, d],
                device_id={"tp": sender},
                device_id_type=MESH,
            ).wait_recv()

    over_group(0, at_all.at[g], at_all.at[g])
    over_tp(0, lambda peer: b_all.at[g, t], b_all.at[g, t])

    over_tp(1, lambda peer: u_all.at[t], u_all.at[t])

    from_group(0, at_all)
    factor = at_all[...].reshape(G * RANK_TILE, CW)
    x_part = x_v[:, pl.ds(pl.multiple_of(t * CW, LANES), CW)]
    r_all[t] = pack_rank(dot_nt(x_part, factor), packed)
    over_tp(2, lambda peer: r_all.at[t], r_all.at[t])

    from_tp(0, b_all.at[g])
    over_group(1, b_all.at[g], b_all.at[g])

    def to_sibling(index, src, dst):
        copy = pltpu.make_async_remote_copy(
            src_ref=src,
            dst_ref=dst,
            send_sem=sib_ssem.at[index],
            recv_sem=sib_rsem.at[index],
            device_id={"tp": sibling},
            device_id_type=MESH,
        )
        copy.start()
        pending.append(copy)

    def from_sibling(index, slot):
        pltpu.make_async_remote_copy(
            src_ref=slot,
            dst_ref=slot,
            send_sem=sib_ssem.at[index],
            recv_sem=sib_rsem.at[index],
            device_id={"tp": sibling},
            device_id_type=MESH,
        ).wait_recv()

    for z in range(chips):
        to_sibling(z, columns(2 * z + 1 - core), wo_pair.at[z, core])

    load_k.wait()
    load_v.wait()
    load_len.wait()
    load_ck.wait()
    load_cv.wait()
    from_tp(1, u_all)
    from_tp(2, r_all)
    rank_inputs = unpack_rank(jnp.sum(r_all[...], axis=0), packed)
    from_group(1, b_all)
    up = jnp.concatenate(
        [
            jnp.concatenate([b_all[i, h] for h in range(T)], axis=1)
            for i in range(G)
        ],
        axis=0,
    )
    adapter = adapter_scale * dot_wide(rank_inputs, up)
    queries = []
    for h in range(T):
        one = (u_all[h] + adapter[:, h * D : (h + 1) * D]).astype(bf16)
        q_all[h] = one
        queries.append(one.astype(f32))

    position = t * block + lax.broadcasted_iota(jnp.int32, (gh * steps, block), 1)
    lane = lax.broadcasted_iota(jnp.int32, (gh * steps, LANES), 1)
    share = LANES // (2 * rows)
    for j in range(kv_heads):
        stat = jnp.zeros((gh * steps, LANES), f32)
        for i in range(rows):
            grouped = jnp.concatenate(
                [
                    queries[h][i * steps : (i + 1) * steps]
                    for h in range(j * gh, (j + 1) * gh)
                ],
                axis=0,
            ).astype(bf16)
            at = (i * kv_heads + j) * block
            scores = dot_nt(grouped, k_v[at : at + block]) * scale
            visible = position < len_s[i]
            peak = jnp.max(
                jnp.where(visible, scores, masked_score), axis=1, keepdims=True
            )
            weights = jnp.where(visible, jnp.exp(scores - peak), 0.0)
            total = jnp.sum(weights, axis=1, keepdims=True)
            outputs = dot_nn(weights.astype(bf16), v_v[at : at + block])
            o_send[j * gh : (j + 1) * gh, i * steps : (i + 1) * steps, :] = (
                outputs.reshape(gh, steps, D)
            )
            stat = jnp.where(
                lane >= 2 * i * share,
                jnp.where(lane >= (2 * i + 1) * share, total, peak),
                stat,
            )
        o_send[j * gh : (j + 1) * gh, R : R + steps, :] = stat.reshape(
            gh, steps, LANES
        )
    over_tp(3, lambda peer: o_send.at[peer], o_recv.at[t])
    o_recv[t] = o_send[t]
    load_oa.wait()
    load_ob.wait()
    over_group(2, oat_pair.at[core, g], oat_pair.at[core, g])
    over_group(3, ob_all.at[g], ob_all.at[g])

    mine = q_all[t]
    fresh_scores = dot_nt(mine, ck_v[...]) * scale
    row_of = lax.broadcasted_iota(jnp.int32, (R, R), 0)
    col_of = lax.broadcasted_iota(jnp.int32, (R, R), 1)
    causal = (lax.div(row_of, steps) == lax.div(col_of, steps)) & (row_of >= col_of)
    fresh_peak = jnp.max(
        jnp.where(causal, fresh_scores, masked_score), axis=1, keepdims=True
    )
    fresh_weights = jnp.where(causal, jnp.exp(fresh_scores - fresh_peak), 0.0)
    fresh_sum = jnp.sum(fresh_weights, axis=1, keepdims=True)
    fresh_out = dot_nn(fresh_weights.astype(bf16), cv_v[...])

    from_group(2, oat_pair.at[core])
    to_sibling(chips, oat_pair.at[core], oat_pair.at[core])
    from_group(3, ob_all)
    for z in range(chips):
        load_wo[z].wait()
        from_sibling(z, wo_pair.at[z, 1 - core])
    from_sibling(chips, oat_pair.at[1 - core])

    from_tp(3, o_recv)
    stats = o_recv[:, R : R + steps, :]
    peaks, sums, outs = [], [], []
    for i in range(rows):
        block_peak = stats[:, :, 2 * i * share : 2 * i * share + 1]
        block_sum = stats[:, :, (2 * i + 1) * share : (2 * i + 1) * share + 1]
        top = jnp.max(block_peak, axis=0)
        rescale = jnp.exp(block_peak - top[None])
        peaks.append(top)
        sums.append(jnp.sum(rescale * block_sum, axis=0))
        outs.append(
            jnp.sum(rescale * o_recv[:, i * steps : (i + 1) * steps, :], axis=0)
        )
    cache_peak = jnp.concatenate(peaks, axis=0)
    cache_sum = jnp.concatenate(sums, axis=0)
    cache_out = jnp.concatenate(outs, axis=0)
    joint = jnp.maximum(cache_peak, fresh_peak)
    left = jnp.exp(cache_peak - joint)
    right = jnp.exp(fresh_peak - joint)
    numer = cache_out * left + fresh_out * right
    denom = cache_sum * left + fresh_sum * right
    ctx_pair[core] = (numer / denom).astype(bf16)

    to_sibling(chips + 1, ctx_pair.at[core], ctx_pair.at[core])
    from_sibling(chips + 1, ctx_pair.at[1 - core])
    context = jnp.concatenate([ctx_pair[0], ctx_pair[1]], axis=1)

    def across(index, j, src, dst):
        copy = pltpu.make_async_remote_copy(
            src_ref=src,
            dst_ref=dst,
            send_sem=p_ssem.at[index, j],
            recv_sem=p_rsem.at[index, j],
            device_id={"tp": 2 * partner(chip, j) + core},
            device_id_type=MESH,
        )
        copy.start()
        pending.append(copy)
        return copy

    rr_own[...] = pack_rank(
        dot_nt(ctx_pair[0], oat_pair[0].reshape(G * RANK_TILE, D))
        + dot_nt(ctx_pair[1], oat_pair[1].reshape(G * RANK_TILE, D)),
        packed,
    )
    ranks = {}
    for j in reversed(range(1, chips)):
        ranks[j] = across(1, j, rr_own, rr_recv.at[j])
    arrivals = {}
    for j in reversed(range(chips)):
        p_send[j] = dot_nn(context, wo_pair[partner(chip, j)].reshape(2 * D, CW))
        if j:
            arrivals[j] = across(0, j, p_send.at[j], p_recv.at[j])
    last = 2 * (chips - 1)
    for copy in pending[: len(pending) - last]:
        copy.wait_send()
    rank_sum = rr_own[...]
    for j in range(1, chips):
        ranks[j].wait_recv()
        rank_sum += rr_recv[j]
    rank_outputs = unpack_rank(rank_sum, packed)
    result = p_send[0] + adapter_scale * dot_wide(
        rank_outputs, ob_all[...].reshape(G * RANK_TILE, CW)
    )
    for j in range(1, chips):
        arrivals[j].wait_recv()
        result += p_recv[j]
    out[...] = result.astype(out.dtype)

    for copy in pending[len(pending) - last :]:
        copy.wait_send()


def padded(value, axis, size):
    if value.shape[axis] == size:
        return value
    widths = [(0, 0)] * value.ndim
    widths[axis] = (0, size - value.shape[axis])
    return jnp.pad(value, widths)


def chunked(value, axis, count, size):
    shape = value.shape
    if shape[axis] == count * size:
        return value
    split = shape[:axis] + (count, shape[axis] // count) + shape[axis + 1 :]
    value = padded(value.reshape(split), axis + 1, size)
    return value.reshape(shape[:axis] + (count * size,) + shape[axis + 1 :])


def on_device(
    decoding_input,
    query_weight,
    output_weight,
    query_down_factor,
    query_up_factor,
    output_down_factor,
    output_up_factor,
    stored_keys,
    stored_values,
    current_keys,
    current_values,
    lengths,
):
    T = lax.axis_size("tp")
    G = lax.axis_size("group")
    rows, steps, width = decoding_input.shape
    kv_heads, block, D = stored_keys.shape[1:]
    assert query_weight.shape[1] == D and T > 1 and T & (T - 1) == 0
    R = rows * steps
    chunk = width // T
    CW = rounded_up(chunk, LANES)
    rank = G * RANK_TILE
    packed = 2 * rank == LANES
    rank_shape = (R // 2, LANES) if packed else (R, rank)

    x = chunked(decoding_input.reshape(R, width), 1, T, CW)
    wq = chunked(query_weight, 0, T, CW)
    wo = chunked(output_weight, 1, T, CW)
    a = padded(padded(query_down_factor.T, 0, RANK_TILE), 1, CW)
    b = padded(query_up_factor, 0, RANK_TILE)
    oa = padded(output_down_factor.T, 0, RANK_TILE)
    ob = padded(padded(output_up_factor, 0, RANK_TILE), 1, CW)
    k = stored_keys.reshape(rows * kv_heads * block, D)
    v = stored_values.reshape(rows * kv_heads * block, D)
    if kv_heads > 1:
        shared = lax.axis_index("tp") // (T // kv_heads)
        current_keys = lax.dynamic_slice_in_dim(current_keys, shared, 1, 2)
        current_values = lax.dynamic_slice_in_dim(current_values, shared, 1, 2)
    ck = current_keys.reshape(R, D)
    cv = current_values.reshape(R, D)

    vmem = pltpu.VMEM
    dma = pltpu.SemaphoreType.DMA
    result = pl.pallas_call(
        functools.partial(kernel, T, G, rows, steps, kv_heads, block, CW, packed),
        out_shape=pltpu.VMEM((R, CW), bf16),
        in_specs=[pl.BlockSpec(memory_space=pltpu.HBM)] * 12,
        out_specs=pl.BlockSpec(memory_space=pltpu.VMEM),
        scratch_shapes=[
            vmem(x.shape, bf16),
            vmem(wq.shape, bf16),
            vmem((T // 2, 2, D, CW), bf16),
            vmem(k.shape, bf16),
            vmem(v.shape, bf16),
            vmem(ck.shape, bf16),
            vmem(cv.shape, bf16),
            pltpu.SMEM(lengths.shape, jnp.int32),
            vmem((G, RANK_TILE, CW), bf16),
            vmem((G, T, RANK_TILE, D), bf16),
            vmem((T, R, D), f32),
            vmem((T,) + rank_shape, f32),
            vmem((2, G, RANK_TILE, D), bf16),
            vmem((G, RANK_TILE, CW), bf16),
            vmem((T, R, D), bf16),
            vmem((T, R + steps, D), f32),
            vmem((T, R + steps, D), f32),
            vmem(rank_shape, f32),
            vmem((T // 2,) + rank_shape, f32),
            vmem((2, R, D), bf16),
            vmem((T // 2, R, CW), f32),
            vmem((T // 2, R, CW), f32),
            dma((11 + T // 2,)),
            dma((4, T)),
            dma((4, T)),
            dma((4, G)),
            dma((4, G)),
            dma((T // 2 + 2,)),
            dma((T // 2 + 2,)),
            dma((2, T // 2)),
            dma((2, T // 2)),
        ],
        compiler_params=pltpu.CompilerParams(
            collective_id=0, has_side_effects=True, vmem_limit_bytes=56 * 2**20
        ),
        cost_estimate=pl.CostEstimate(
            flops=4 * R * width * D, bytes_accessed=4 * width * D, transcendentals=0
        ),
    )(x, wq, wo, a, b, oa, ob, k, v, ck, cv, lengths)
    return result[:, :chunk].reshape(rows, steps, chunk)


def solution(mesh):
    in_specs = (
        P("group", None, None),
        P(None, "tp"),
        P("tp", None),
        P("tp", "group"),
        P("group", "tp"),
        P("tp", "group"),
        P("group", "tp"),
        P("group", None, "tp", None),
        P("group", None, "tp", None),
        P("group", None, None, None),
        P("group", None, None, None),
        P("group"),
    )
    out_specs = P("group", None, "tp")
    return jax.shard_map(
        on_device, mesh=mesh, in_specs=in_specs, out_specs=out_specs, check_vma=False
    )
```
